256 devices in a mesh: row: 64 (over y, z, core), cand: 4 (over x).
Axes of the slice: x: 4, y: 4, z: 8, core: 2. Of those that a mesh axis runs over, the one named last changes fastest.
Arguments:
- cross_cov: float32 [65536, 4096], P('row', 'cand'), may hold values from -3 to 3
- factor_cols: float32 [65536, 1024], P('row'), as said below
- prior_cov: float32 [4096, 4096], P('row', 'cand'), may hold values from -6 to 6
Outputs:
- solved_rhs: float32 [65536, 4096], P('row', 'cand')
- posterior_cov: float32 [4096, 4096], P('row', 'cand')
The draws below stay inside these ranges and needn't reach their ends.
Inputs may be any that keep to these rules, and one draw needn't show every extreme that they name: In block s, the entries of factor_cols at row s * 1024 + i and column s * 256 + i (the diagonal of D_s) lie between 1 and 2.
All inputs are finite; a program needn't handle non-finite values.
Results may differ from the reference program's by a relative error of at most 0.0001.
Values sent between devices are 32-bit elements; how exact they have to be, the bound alone decides.
A program may use at most 128 MiB of HBM per device.

```python
import jax
import jax.numpy as jnp
from jax import lax

CANDS = 4096
PANEL = 256
STEPS = 4
ROWS_DEV = 1024
WINDOW = 65536


def draw_factor_cols(key, part):
    key = jax.random.fold_in(key, 7)
    first_key, second_key = jax.random.split(key)
    shape = (WINDOW, STEPS * PANEL)
    position = jnp.arange(WINDOW, dtype=jnp.int32)[:, None]
    column = jnp.arange(STEPS * PANEL, dtype=jnp.int32)[None, :]
    owner = position // ROWS_DEV
    within = position % ROWS_DEV
    which_block = column // PANEL
    inner = column % PANEL
    in_diagonal = (owner == which_block) & (within < PANEL)
    noise = jnp.clip(jax.random.normal(first_key, shape, jnp.float32), -4.0, 4.0)
    leading_value = jax.random.uniform(second_key, shape, jnp.float32, minval=1.0, maxval=2.0)
    inside = jnp.where(within == inner, leading_value, 0.7 / PANEL ** 0.5 * noise)
    below = 0.5 / (STEPS * PANEL) ** 0.5 * noise
    return jnp.where(in_diagonal, inside, below).astype(jnp.float32)


def block_scale(stream_key, extent, cuts, smallest, top_value):
    gain = 1.0
    for axis_at, shards_of in cuts:
        steps = jax.random.uniform(jax.random.fold_in(jax.random.fold_in(stream_key, 6), axis_at), (shards_of,), jnp.float32, smallest / len(cuts), top_value / len(cuts))
        gain = gain * jnp.repeat(jnp.exp(steps), extent[axis_at] // shards_of).reshape((-1,) + (1,) * (len(extent) - 1 - axis_at))
    return gain


def scatter_about(key, shape, width, bound, cuts=(), kind=jnp.bfloat16):
    level = block_scale(key, shape, cuts, -0.22, 0.18) if cuts else 1.0
    array = jax.random.normal(key, shape, jnp.float32) * width * level
    return jnp.minimum(jnp.maximum(array, -bound), bound).astype(kind)


def setup_inputs(seed: int = 0) -> dict:
    splits = jax.random.split(jax.random.key(seed), 4)
    return {
        "cross_cov": scatter_about(splits[0], (WINDOW, CANDS), 0.2, 3.0, ((0, 64), (1, 4)), jnp.float32),
        "factor_cols": draw_factor_cols(jax.random.fold_in(splits[3], 71), 0),
        "prior_cov": scatter_about(splits[2], (CANDS, CANDS), 1.0, 6.0, ((0, 64), (1, 4)), jnp.float32),
    }


def reference(cross_cov, factor_cols, prior_cov):
    highest_precision = lax.Precision.HIGHEST
    row_total = cross_cov.shape[0]
    position = jnp.arange(row_total, dtype=jnp.int32)[:, None]
    owner = position // ROWS_DEV
    leading = position % ROWS_DEV < PANEL
    current = cross_cov
    solutions = []
    for section in range(STEPS):
        start = section * ROWS_DEV
        factor_block = factor_cols[:, section * PANEL:(section + 1) * PANEL]
        diagonal = factor_block[start:start + PANEL]
        solution = lax.linalg.triangular_solve(diagonal, current[start:start + PANEL], left_side=True, lower=True)
        update = jnp.dot(factor_block.astype(jnp.float32), solution.astype(jnp.float32), precision=highest_precision, preferred_element_type=jnp.float32)
        finished = leading & (owner <= section)
        current = jnp.where(finished, current, current - update)
        current = current.at[start:start + PANEL].set(solution)
        solutions.append(solution)
    stacked = jnp.concatenate(solutions, axis=0)
    downdate = lax.dot_general(stacked.astype(jnp.float32), stacked.astype(jnp.float32), (((0,), (0,)), ((), ())), precision=highest_precision, preferred_element_type=jnp.float32)
    return (current, prior_cov - downdate)
```

```python
import functools

import jax
import jax.numpy as jnp
from jax import lax
from jax.experimental import pallas as pl
from jax.experimental.pallas import tpu as pltpu
from jax.sharding import PartitionSpec as P

MESH = pl.DeviceIdType.MESH
F32, BF16 = jnp.float32, jnp.bfloat16
HIGHEST = lax.Precision.HIGHEST
B = 256
SUB = 1
PIECE = 64 // SUB
LAG = 2
DPOS = 1

TREES = (
    (2, 112, 98, 82, 74, 62, 46, 22, 48, 96, 112, 98, 86, 66, 48, 37, 65, 93, 96, 112, 98, 81, 96, 49, 80, 96, 112, 98, 82, 72, 49, 65),
    (1, 21, 45, 61, 69, 81, 97, 112, 48, 38, 48, 64, 81, 97, 112, 96, 66, 50, 96, 82, 97, 112, 96, 94, 80, 66, 50, 73, 89, 97, 112, 96),
    (8, 48, 64, 80, 96, 80, 64, 48, 48, 96, 82, 96, 112, 96, 81, 96, 40, 48, 73, 88, 104, 90, 74, 48, 27, 45, 61, 68, 84, 70, 62, 46),
    (4, 56, 64, 80, 96, 80, 64, 56, 23, 41, 61, 77, 88, 76, 62, 42, 36, 80, 70, 85, 100, 84, 69, 80, 48, 64, 80, 96, 112, 96, 80, 64),
)
STEP = ((0, 1), (0, 7), (1, 0), (3, 0))
FIRST = (1, 0, 3, 2)
NL = (1, 5)
NB = (11, 15)
BASE = (0, 11)
BLOCKS = 26
LOWER = (((1, 0),), ((3, 2), (2, 0), (3, 0), (2, 1), (3, 1)))
DEPTH = 7
UNITS = NB[1] * SUB + LAG * DEPTH


def b_index(q, s):
    rho, half = s // 2, s % 2
    return BASE[rho] + NL[rho] + 2 * q + half + jnp.where(q >= DPOS, 2, 0)


def d_index(s):
    rho, half = s // 2, s % 2
    return BASE[rho] + NL[rho] + 2 * DPOS + half


def l_index(s, t):
    rho = s // 2
    return BASE[rho] + LOWER[rho].index((s, t))


def split(x):
    hi = x.astype(BF16)
    return hi, (x - hi.astype(F32)).astype(BF16)


def dot(a, b):
    return jnp.dot(a, b, preferred_element_type=F32)


def dot3(ah, al, bh, bl):
    return dot(ah, bh) + (dot(ah, bl) + dot(al, bh))


def dotf(a, b):
    return jnp.dot(a, b, precision=HIGHEST, preferred_element_type=F32)


def invert_lower(d):
    ri = lax.broadcasted_iota(jnp.int32, (B, B), 0)
    ci = lax.broadcasted_iota(jnp.int32, (B, B), 1)
    same = ri == ci
    on_diag = jnp.where(same, d, 0.0)
    by_row = 1.0 / jnp.sum(on_diag, axis=1, keepdims=True)
    by_col = 1.0 / jnp.sum(on_diag, axis=0, keepdims=True)
    n = jnp.where(ri > ci, d, 0.0) * by_row
    inv = jnp.where(same, 1.0, 0.0) - jnp.where((ri >> 1) == (ci >> 1), n, 0.0)
    for k in range(1, 8):
        off = jnp.where(((ri >> (k + 1)) == (ci >> (k + 1))) & ((ri >> k) != (ci >> k)), n, 0.0)
        inv = inv - dotf(dotf(inv, off), inv)
    return inv * by_col


def kernel(
    c_hbm, f_hbm, p_hbm, out_hbm, post_hbm,
    w, fv, fh, fl, cv, pv, xh, xl, lh, ll, dv, xb, sbt, tv,
    rs, sb, child_sem, sib_sem, own_sem, load_sem, raw_sem, out_sem, xr, xs, xsb, xss,
):
    row = lax.axis_index("row")
    x = lax.axis_index("cand")
    y = row // 16
    z = (row // 2) % 8
    core = row % 2

    def device(yy, zz, cc, xx=None):
        return ((yy % 4) * 16 + (zz % 8) * 2 + cc, x if xx is None else xx % 4)

    sibling = device(y, z, 1 - core)

    def towards(d, cc):
        return device(y + STEP[d][0], z + STEP[d][1], cc)

    load_f = pltpu.make_async_copy(f_hbm, fv, load_sem.at[0])
    load_c = pltpu.make_async_copy(c_hbm, cv, load_sem.at[1])
    load_p = pltpu.make_async_copy(p_hbm, pv, load_sem.at[2])

    def raw_blocks(s):
        found = []
        for t in range(s):
            found.append((l_index(s, t), f_hbm.at[pl.ds(0, B), pl.ds(t * B, B)]))
        for q in range(4):
            b = BASE[s // 2] + NL[s // 2] + 2 * q + s % 2 + (2 if q >= DPOS else 0)
            found.append((b, c_hbm.at[pl.ds(0, B), pl.ds(q * B, B)]))
        return sorted(found, key=lambda e: e[0])

    for s in range(4):

        @pl.when(row == s)
        def _(s=s):
            pltpu.make_async_copy(f_hbm.at[pl.ds(0, B), pl.ds(s * B, B)], dv, raw_sem.at[7]).start()
            for i, (b, src) in enumerate(raw_blocks(s)):
                pltpu.make_async_copy(src, w.at[b], raw_sem.at[i]).start()

    barrier = pltpu.get_barrier_semaphore()
    for d in range(4):
        for cc in range(2):
            pl.semaphore_signal(barrier, inc=1, device_id=towards(d, cc), device_id_type=MESH)
    for dx in (1, 3):
        pl.semaphore_signal(barrier, inc=1, device_id=device(y, z, core, x + dx), device_id_type=MESH)
    pl.semaphore_signal(barrier, inc=1, device_id=sibling, device_id_type=MESH)
    load_f.start()
    load_c.start()
    load_p.start()
    pl.semaphore_wait(barrier, 11)

    def own_copies(s, b, slot):
        copies = []
        for tree in range(4):
            for k in range(SUB):
                rows = w.at[b, pl.ds(64 * tree + PIECE * k, PIECE)]
                for other in range(2):
                    if other:
                        sem = (rs if tree // 2 != s % 2 else sb).at[b * SUB + k, tree % 2]
                        to = sibling
                    else:
                        sem = rs.at[b * SUB + k, tree % 2]
                        to = towards(FIRST[tree], tree // 2)
                    copies.append(
                        pltpu.make_async_remote_copy(
                            src_ref=rows, dst_ref=rows, send_sem=own_sem.at[slot, (tree * SUB + k) * 2 + other],
                            recv_sem=sem, device_id=to, device_id_type=MESH,
                        )
                    )
        return copies

    def own_blocks(s):
        found = [b for b, _ in raw_blocks(s)]
        return found

    for s in range(4):

        @pl.when(row == s)
        def _(s=s):
            d_block = BASE[s // 2] + NL[s // 2] + 2 * DPOS + s % 2
            blocks = raw_blocks(s)
            done = False
            for i, (b, src) in enumerate(blocks):
                pltpu.make_async_copy(src, w.at[b], raw_sem.at[i]).wait()
            first = [i for i, (b, _) in enumerate(blocks) if b < d_block]
            later = [i for i, (b, _) in enumerate(blocks) if b > d_block]
            for i in first:
                for c in own_copies(s, blocks[i][0], i):
                    c.start()
            pltpu.make_async_copy(f_hbm.at[pl.ds(0, B), pl.ds(s * B, B)], dv, raw_sem.at[7]).wait()
            w[d_block] = invert_lower(dv[...])
            for c in own_copies(s, d_block, 7):
                c.start()
            for i in later:
                for c in own_copies(s, blocks[i][0], i):
                    c.start()

    load_f.wait()

    @pl.loop(0, 16)
    def _(i):
        rows = pl.ds(pl.multiple_of(i * 64, 64), 64)
        hi, lo = split(fv[rows, :])
        fh[rows, :] = hi
        fl[rows, :] = lo

    def lookup(table, key):
        found = jnp.int32(0)
        for k, v in enumerate(table):
            found = jnp.where(key == k, v, found)
        return found

    place = []
    for rho in range(2):
        idx = y * 8 + (z - rho + 8) % 8
        merged = [TREES[2 * cc][k] + 128 * TREES[2 * cc + 1][k] for cc in range(2) for k in range(32)]
        v = lookup(merged, core * 32 + idx)
        place.append((idx == 0, (v % 128, v // 128)))

    def piece(b, k, rows_tree):
        return w.at[b, pl.ds(pl.multiple_of(rows_tree * 64 + k * PIECE, 8), PIECE)]

    def forward(rho, il, n):
        is_root, values = place[rho]
        mask = values[il] % 16
        block_n = n // SUB
        b = BASE[rho] + block_n
        k = n % SUB
        ref = piece(b, k, 2 * core + il)
        sem_i = b * SUB + k

        @pl.when(jnp.logical_or(jnp.logical_not(is_root), (block_n + 1) % 2 != core))
        def _():
            pltpu.make_async_remote_copy(
                src_ref=ref, dst_ref=ref, send_sem=sib_sem.at[rho, il], recv_sem=rs.at[sem_i, il],
                device_id=sibling, device_id_type=MESH,
            ).wait_recv()

        @pl.when(jnp.logical_not(is_root))
        def _():
            for d in range(4):

                @pl.when((mask // 2**d) % 2 == 1)
                def _(d=d):
                    pltpu.make_async_remote_copy(
                        src_ref=ref, dst_ref=ref, send_sem=child_sem.at[rho, il, d], recv_sem=rs.at[sem_i, il],
                        device_id=towards(d, core), device_id_type=MESH,
                    ).start()

            pltpu.make_async_remote_copy(
                src_ref=ref, dst_ref=ref, send_sem=sib_sem.at[rho, il], recv_sem=sb.at[sem_i, il],
                device_id=sibling, device_id_type=MESH,
            ).start()

    def step(u, carry):
        for rho in range(2):
            for il in range(2):
                n = u - LAG * (place[rho][1][il] // 16)

                @pl.when(jnp.logical_and(n >= 0, n < NB[rho] * SUB))
                def _(rho=rho, il=il, n=n):
                    forward(rho, il, n)

        return carry

    lax.fori_loop(0, UNITS, step, 0)

    p = (x - y + 4) % 4
    qz = z // 2
    half = pl.ds(pl.multiple_of(core * 128, 128), 128)
    lanes = pl.ds(pl.multiple_of((z % 2) * 128, 128), 128)

    def x_copy(s, dx, src, slot):
        return pltpu.make_async_remote_copy(
            src_ref=src, dst_ref=xb.at[s, half], send_sem=xs.at[slot, s], recv_sem=xr.at[s],
            device_id=device(y, z, core, x + dx), device_id_type=MESH,
        )

    def x_sibling(s):
        return pltpu.make_async_remote_copy(
            src_ref=xb.at[s, half], dst_ref=xb.at[s, half], send_sem=xss.at[s], recv_sem=xsb.at[s],
            device_id=sibling, device_id_type=MESH,
        )

    def x_source(s):
        return w.at[b_index(qz, s), half, lanes]

    @pl.when(p == 0)
    def _():
        for s in range(4):
            x_copy(s, 1, x_source(s), 0).start()
            x_copy(s, 3, x_source(s), 1).start()

    relays = jnp.logical_or(jnp.logical_and(p == 1, core == 0), jnp.logical_and(p == 3, core == 1))
    onward = jnp.where(core == 0, 1, 3)

    def x_relay():
        for s in range(4):
            x_copy(s, 1, x_source(s), 0).wait_recv()

            @pl.when(relays)
            def _(s=s):
                x_copy(s, onward, xb.at[s, half], 0).start()

            x_sibling(s).start()

    def wait_other(b, rho, block_n):
        is_root = place[rho][0]

        @pl.when(jnp.logical_or(jnp.logical_not(is_root), (block_n + 1) % 2 != core))
        def _():
            for il in range(2):
                for k in range(SUB):
                    ref = piece(b, k, 2 * (1 - core) + il)
                    pltpu.make_async_remote_copy(
                        src_ref=ref, dst_ref=ref, send_sem=sib_sem.at[rho, il], recv_sem=sb.at[b * SUB + k, il],
                        device_id=sibling, device_id_type=MESH,
                    ).wait_recv()

    for s in range(4):
        for t in range(s):
            b = l_index(s, t)
            wait_other(b, s // 2, b - BASE[s // 2])
            hi, lo = split(w[b])
            lh[s * (s - 1) // 2 + t] = hi
            ll[s * (s - 1) // 2 + t] = lo
        b = BASE[s // 2] + NL[s // 2] + 2 * DPOS + s % 2
        wait_other(b, s // 2, b - BASE[s // 2])
        hi, lo = split(w[b])
        lh[6 + s] = hi
        ll[6 + s] = lo

    def solve(load, store):
        parts = []
        for s in range(4):
            r = load(s)
            for t in range(s):
                i = s * (s - 1) // 2 + t
                r = r - dot3(lh[i], ll[i], *parts[t])
            v = dot3(lh[6 + s], ll[6 + s], *split(r))
            parts.append(split(v))
            store(s, v, *parts[s])

    load_c.wait()

    def group(q):
        cols = pl.ds(pl.multiple_of(q * B, B), B)
        for s in range(4):
            b = b_index(q, s)
            wait_other(b, s // 2, b - BASE[s // 2])

        def store(s, v, hi, lo):
            xh[pl.ds(s * B, B), cols] = hi
            xl[pl.ds(s * B, B), cols] = lo

            @pl.when(row == s)
            def _():
                dv[...] = v

        solve(lambda s: w[b_index(q, s)], store)
        for m in range(4):
            rows = pl.ds(m * B, B)
            cv[rows, cols] = cv[rows, cols] - dot3(fh[rows, :], fl[rows, :], xh[:, cols], xl[:, cols])

        @pl.when(row < 4)
        def _():
            cv[pl.ds(0, B), cols] = dv[...]

        pltpu.make_async_copy(cv.at[:, cols], out_hbm.at[:, cols], out_sem.at[q]).start()

    @pl.loop(0, 4)
    def _(q):
        group(q)

        @pl.when(jnp.logical_and(q == 1, jnp.logical_or(p == 1, p == 3)))
        def _():
            x_relay()

        @pl.when(jnp.logical_and(q == 2, p == 2))
        def _():
            x_relay()

    @pl.when(p == 0)
    def _():
        for s in range(4):
            xb[s] = w[b_index(qz, s), :, lanes]

    @pl.when(p != 0)
    def _():
        for s in range(4):
            other = xb.at[s, pl.ds(pl.multiple_of((1 - core) * 128, 128), 128)]
            pltpu.make_async_remote_copy(
                src_ref=other, dst_ref=other, send_sem=xss.at[s], recv_sem=xsb.at[s],
                device_id=sibling, device_id_type=MESH,
            ).wait_recv()

    def store_t(s, v, hi, lo):
        sbt[:, pl.ds(s * B, B)] = v.T

    solve(lambda s: xb[s], store_t)
    load_p.wait()
    sh, sl = split(sbt[pl.ds(pl.multiple_of(core * 64, 64), 64), :])

    for q in range(4):
        cols = pl.ds(q * B, B)
        tv[:, cols] = pv[:, cols] - dot3(sh, sl, xh[:, cols], xl[:, cols])

    save_p = pltpu.make_async_copy(tv, post_hbm, out_sem.at[4])
    save_p.start()

    for s in range(4):

        @pl.when(row == s)
        def _(s=s):
            for i, (b, _) in enumerate(raw_blocks(s)):
                for c in own_copies(s, b, i):
                    c.wait_send()
            for c in own_copies(s, BASE[s // 2] + NL[s // 2] + 2 * DPOS + s % 2, 7):
                c.wait_send()

    for rho in range(2):
        is_root, values = place[rho]
        whole = w.at[pl.ds(0, NB[rho]), pl.ds(0, 64)]

        @pl.when(jnp.logical_not(is_root))
        def _(rho=rho, values=values, whole=whole):
            for il in range(2):
                for d in range(4):

                    @pl.when((values[il] % 16 // 2**d) % 2 == 1)
                    def _(il=il, d=d):
                        pltpu.make_async_remote_copy(
                            src_ref=whole, dst_ref=whole, send_sem=child_sem.at[rho, il, d], recv_sem=rs.at[0, il],
                            device_id=towards(d, core), device_id_type=MESH,
                        ).wait_send()

                pltpu.make_async_remote_copy(
                    src_ref=whole, dst_ref=whole, send_sem=sib_sem.at[rho, il], recv_sem=rs.at[0, il],
                    device_id=sibling, device_id_type=MESH,
                ).wait_send()

    @pl.when(p == 0)
    def _():
        for s in range(4):
            x_copy(s, 1, x_source(s), 0).wait_send()
            x_copy(s, 3, x_source(s), 1).wait_send()

    @pl.when(p != 0)
    def _():
        for s in range(4):

            @pl.when(relays)
            def _(s=s):
                x_copy(s, onward, xb.at[s, half], 0).wait_send()

            x_sibling(s).wait_send()

    save_p.wait()
    for q in range(4):
        cols = pl.ds(q * B, B)
        pltpu.make_async_copy(cv.at[:, cols], out_hbm.at[:, cols], out_sem.at[q]).wait()


def local(cross_cov, factor_cols, prior_cov):
    n = 1024
    dma = pltpu.SemaphoreType.DMA
    any_space = pl.BlockSpec(memory_space=pl.ANY)
    return pl.pallas_call(
        kernel,
        out_shape=(jax.ShapeDtypeStruct((n, n), F32), jax.ShapeDtypeStruct((64, n), F32)),
        in_specs=[any_space] * 3,
        out_specs=(any_space, any_space),
        scratch_shapes=[
            pltpu.VMEM((BLOCKS, B, B), F32),
            pltpu.VMEM((n, n), F32),
            pltpu.VMEM((n, n), BF16),
            pltpu.VMEM((n, n), BF16),
            pltpu.VMEM((n, n), F32),
            pltpu.VMEM((64, n), F32),
            pltpu.VMEM((n, n), BF16),
            pltpu.VMEM((n, n), BF16),
            pltpu.VMEM((10, B, B), BF16),
            pltpu.VMEM((10, B, B), BF16),
            pltpu.VMEM((B, B), F32),
            pltpu.VMEM((4, B, 128), F32),
            pltpu.VMEM((128, n), F32),
            pltpu.VMEM((64, n), F32),
            dma((BLOCKS * SUB, 2)),
            dma((BLOCKS * SUB, 2)),
            dma((2, 2, 4)),
            dma((2, 2)),
            dma((8, 8 * SUB)),
            dma((3,)),
            dma((8,)),
            dma((5,)),
            dma((4,)),
            dma((2, 4)),
            dma((4,)),
            dma((4,)),
        ],
        compiler_params=pltpu.CompilerParams(
            collective_id=0, has_side_effects=True, vmem_limit_bytes=56 * 1024 * 1024
        ),
        name="solve_update",
    )(cross_cov, factor_cols, prior_cov)


def solution(mesh):
    placed = (P("row", "cand"), P("row", None), P("row", "cand"))
    return jax.shard_map(
        local,
        mesh=mesh,
        in_specs=placed,
        out_specs=(P("row", "cand"), P("row", "cand")),
        check_vma=False,
    )
```

```python
import functools

import jax
import jax.numpy as jnp
from jax import lax
from jax.experimental import pallas as pl
from jax.experimental.pallas import tpu as pltpu
from jax.sharding import PartitionSpec as P

MESH = pl.DeviceIdType.MESH
F32, BF16 = jnp.float32, jnp.bfloat16
HIGHEST = lax.Precision.HIGHEST
B = 256
PIECE = 64
LAG = 2

TREES = (
    (2, 112, 98, 82, 74, 62, 46, 22, 48, 96, 112, 98, 86, 66, 48, 37, 65, 93, 96, 112, 98, 81, 96, 49, 80, 96, 112, 98, 82, 72, 49, 65),
    (1, 21, 45, 61, 69, 81, 97, 112, 48, 38, 48, 64, 81, 97, 112, 96, 66, 50, 96, 82, 97, 112, 96, 94, 80, 66, 50, 73, 89, 97, 112, 96),
    (8, 48, 64, 80, 96, 80, 64, 48, 48, 96, 82, 96, 112, 96, 81, 96, 40, 48, 73, 88, 104, 90, 74, 48, 27, 45, 61, 68, 84, 70, 62, 46),
    (4, 56, 64, 80, 96, 80, 64, 56, 23, 41, 61, 77, 88, 76, 62, 42, 36, 80, 70, 85, 100, 84, 69, 80, 48, 64, 80, 96, 112, 96, 80, 64),
)
STEP = ((0, 1), (0, 7), (1, 0), (3, 0))
FIRST = (1, 0, 3, 2)
NL = (0, 4)
NB = (8, 12)
BASE = (0, 8)
BLOCKS = 20
WAIT = LAG * 7
START = NL[1] + 1
UNITS = NB[1] + WAIT + 4


def b_index(q, s):
    return BASE[s // 2] + NL[s // 2] + 2 * q + s % 2


def split(x):
    hi = x.astype(BF16)
    return hi, (x - hi.astype(F32)).astype(BF16)


def dot(a, b):
    return jnp.dot(a, b, preferred_element_type=F32)


def dot3(ah, al, bh, bl):
    return dot(ah, bh) + (dot(ah, bl) + dot(al, bh))


def dotf(a, b):
    return jnp.dot(a, b, precision=HIGHEST, preferred_element_type=F32)


def invert_lower(d):
    ri = lax.broadcasted_iota(jnp.int32, (B, B), 0)
    ci = lax.broadcasted_iota(jnp.int32, (B, B), 1)
    same = ri == ci
    on_diag = jnp.where(same, d, 0.0)
    by_row = 1.0 / jnp.sum(on_diag, axis=1, keepdims=True)
    by_col = 1.0 / jnp.sum(on_diag, axis=0, keepdims=True)
    n = jnp.where(ri > ci, d, 0.0) * by_row
    inv = jnp.where(same, 1.0, 0.0) - jnp.where((ri >> 1) == (ci >> 1), n, 0.0)
    for k in range(1, 8):
        off = jnp.where(((ri >> (k + 1)) == (ci >> (k + 1))) & ((ri >> k) != (ci >> k)), n, 0.0)
        inv = inv - dotf(dotf(inv, off), inv)
    return inv * by_col


def kernel(
    c_hbm, f_hbm, p_hbm, out_hbm, post_hbm,
    w, fv, fh, fl, cv, pv, xh, xl, gh, gl, dsp, dv, lv, xb, sbt, tv,
    rs, sb, child_sem, sib_sem, own_sem, pre_s, pre_r, load_sem, raw_sem, out_sem, xr, xs, xsb, xss,
):
    row = lax.axis_index("row")
    x = lax.axis_index("cand")
    y = row >> 4
    z = (row >> 1) & 7
    core = row & 1

    def device(yy, zz, cc, xx=None):
        return ((yy & 3) * 16 + (zz & 7) * 2 + cc, x if xx is None else xx & 3)

    sibling = device(y, z, 1 - core)
    near = [[device(y + dy, z + dz, cc) for cc in range(2)] for dy, dz in STEP]
    near_same = [device(y + dy, z + dz, core) for dy, dz in STEP]
    beside = [device(y, z, core, x + dx) for dx in (1, 3)]

    def remote(src, dst, send_sem, recv_sem, to):
        return pltpu.make_async_remote_copy(
            src_ref=src, dst_ref=dst, send_sem=send_sem, recv_sem=recv_sem, device_id=to, device_id_type=MESH
        )

    load_f = pltpu.make_async_copy(f_hbm, fv, load_sem.at[0])
    load_c = pltpu.make_async_copy(c_hbm, cv, load_sem.at[1])
    load_p = pltpu.make_async_copy(p_hbm, pv, load_sem.at[2])

    def raw_copies(s):
        found = [(w.at[b_index(q, s)], c_hbm.at[pl.ds(0, B), pl.ds(q * B, B)]) for q in range(4)]
        for t in range(2 if s >= 2 else 0):
            found.append((w.at[BASE[1] + 2 * t + s % 2], f_hbm.at[pl.ds(0, B), pl.ds(t * B, B)]))
        if s % 2:
            found.append((lv, f_hbm.at[pl.ds(0, B), pl.ds((s - 1) * B, B)]))
        return [pltpu.make_async_copy(src, dst, raw_sem.at[i]) for i, (dst, src) in enumerate(found)]

    def load_d(s):
        return pltpu.make_async_copy(f_hbm.at[pl.ds(0, B), pl.ds(s * B, B)], dv, raw_sem.at[7])

    for s in range(4):

        @pl.when(row == s)
        def _(s=s):
            load_d(s).start()
            for c in raw_copies(s):
                c.start()

    barrier = pltpu.get_barrier_semaphore()
    for to in [t for pair in near for t in pair] + beside + [sibling]:
        pl.semaphore_signal(barrier, inc=1, device_id=to, device_id_type=MESH)
    load_f.start()
    load_c.start()
    load_p.start()

    for s in range(4):

        @pl.when(row == s)
        def _(s=s):
            load_d(s).wait()
            dsp[0], dsp[1] = split(invert_lower(dv[...]))
            for c in raw_copies(s):
                c.wait()
            if s % 2:
                dsp[2], dsp[3] = split(lv[...])

    def lookup(table, key):
        found = jnp.int32(0)
        for k, v in enumerate(table):
            found = jnp.where(key == k, v, found)
        return found

    is_root, depth, child = [], [], []
    for rho in range(2):
        idx = y * 8 + ((z - rho) & 7)
        merged = [TREES[2 * cc][k] + 128 * TREES[2 * cc + 1][k] for cc in range(2) for k in range(32)]
        v = lookup(merged, core * 32 + idx)
        is_root.append(idx == 0)
        depth.append(((v >> 4) & 7, v >> 11))
        child.append((v & 15, (v >> 7) & 15))

    p = (x - y) & 3
    qz = z >> 1
    lanes = pl.ds(pl.multiple_of((z & 1) * 128, 128), 128)
    relays = jnp.logical_or(jnp.logical_and(p == 1, core == 0), jnp.logical_and(p == 3, core == 1))
    onward = (beside[0][0], (x + jnp.where(core == 0, 1, 3)) & 3)
    x_lag = jnp.where(p == 2, 4, 2)

    pl.semaphore_wait(barrier, 11)

    def piece(b, tree):
        return w.at[b, pl.ds(pl.multiple_of(tree * 64, 64), PIECE)]

    def x_piece(s, tree):
        return xb.at[s, pl.ds(pl.multiple_of(tree * 64, 64), PIECE)]

    def needed(rho, n):
        m = n - NL[rho]
        return jnp.logical_and(m >= 0, (m >> 1) == qz), 2 * rho + (m & 1)

    def x_start(rho, il, n):
        hit, s = needed(rho, n)

        @pl.when(jnp.logical_and(p == 0, hit))
        def _():
            tree = 2 * core + il
            src = w.at[BASE[rho] + n, pl.ds(pl.multiple_of(tree * 64, 64), PIECE), lanes]
            for i in range(2):
                remote(src, x_piece(s, tree), xs.at[i, s, il], xr.at[s, il], beside[i]).start()

    def x_arrive(rho, il, n):
        hit, s = needed(rho, n)

        @pl.when(jnp.logical_and(p != 0, hit))
        def _():
            ref = x_piece(s, 2 * core + il)
            remote(ref, ref, xs.at[0, s, il], xr.at[s, il], sibling).wait_recv()

            @pl.when(relays)
            def _():
                remote(ref, ref, xs.at[0, s, il], xr.at[s, il], onward).start()

            remote(ref, ref, xss.at[s, il], xsb.at[s, il], sibling).start()

    def whole_copy(b, n):
        ref = w.at[b]
        return remote(ref, ref, pre_s.at[n >> 1], pre_r.at[n >> 1], sibling)

    def own_sends(b, slot):
        for tree in range(4):
            ref = w.at[b, pl.ds(64 * tree, PIECE)]
            yield remote(ref, ref, own_sem.at[slot, tree], rs.at[b, tree % 2], near[FIRST[tree]][tree // 2])

    def own_wait(slot):
        for copy in own_sends(0, slot):
            copy.wait_send()

    def own(rho, n):
        b = BASE[rho] + n
        j = n >> 1
        slot = j & 1

        @pl.when(core == 1)
        def _():
            whole_copy(b - 1, n).wait_recv()
            for il in range(2):
                x_start(rho, il, n - 1)
            w[b] = w[b] - dot3(dsp[2], dsp[3], *split(w[b - 1]))

        w[b] = dot3(dsp[0], dsp[1], *split(w[b]))
        whole_copy(b, n).start()

        @pl.when(j >= 2)
        def _():
            own_wait(slot)

        for copy in own_sends(b, slot):
            copy.start()
        for il in range(2):
            x_start(rho, il, n)

    def own_other(rho, n):
        whole_copy(BASE[rho] + n, n).wait_recv()
        for il in range(2):
            x_start(rho, il, n)

    def forward(rho, il, n):
        b = BASE[rho] + n
        ref = piece(b, 2 * core + il)
        remote(ref, ref, sib_sem.at[rho, il], rs.at[b, il], sibling).wait_recv()
        for d in range(4):

            @pl.when(((child[rho][il] >> d) & 1) == 1)
            def _(d=d):
                remote(ref, ref, child_sem.at[rho, il, d], rs.at[b, il], near_same[d]).start()

    def share(rho, il, n):
        b = BASE[rho] + n
        ref = piece(b, 2 * core + il)
        remote(ref, ref, sib_sem.at[rho, il], sb.at[b, il], sibling).start()
        x_start(rho, il, n)

    def wait_other(rho, n):
        b = BASE[rho] + n

        @pl.when(jnp.logical_not(is_root[rho]))
        def _():
            for il in range(2):
                ref = piece(b, 2 * (1 - core) + il)
                remote(ref, ref, sib_sem.at[rho, il], sb.at[b, il], sibling).wait_recv()

    def take_g(n):
        wait_other(1, n)
        half, t = n % 2, n // 2
        rows, cols = pl.ds(half * B, B), pl.ds(t * B, B)
        gh[rows, cols], gl[rows, cols] = split(w[BASE[1] + n])

    def finish(y2, y3, hi, lo):
        r = dot3(gh[...], gl[...], hi, lo)
        return y2 - r[:B], y3 - r[B:]

    def columns(q):
        return pl.ds(pl.multiple_of(q * B, B), B)

    def solve_group(q):
        cols = columns(q)
        for s in range(4):
            wait_other(s // 2, b_index(q, s) - BASE[s // 2])
        first = [w[b_index(q, s)] for s in range(2)]
        for s in range(2):
            xh[pl.ds(s * B, B), cols], xl[pl.ds(s * B, B), cols] = split(first[s])
        top = pl.ds(0, 2 * B)
        last = finish(w[b_index(q, 2)], w[b_index(q, 3)], xh[top, cols], xl[top, cols])
        for s in range(2, 4):
            xh[pl.ds(s * B, B), cols], xl[pl.ds(s * B, B), cols] = split(last[s - 2])
        for s, v in enumerate([*first, *last]):

            @pl.when(row == s)
            def _(v=v):
                dv[...] = v

    def update_group(q, part):
        cols = columns(q)
        for m in range(2 * part, 2 * part + 2):
            rows = pl.ds(m * B, B)
            cv[rows, cols] = cv[rows, cols] - dot3(fh[rows, :], fl[rows, :], xh[:, cols], xl[:, cols])

        if part == 0:

            @pl.when(row < 4)
            def _():
                cv[pl.ds(0, B), cols] = dv[...]

        else:
            pltpu.make_async_copy(cv.at[:, cols], out_hbm.at[:, cols], out_sem.at[q]).start()

    def step(u, carry):
        for rho in range(2):

            @pl.when(jnp.logical_and(is_root[rho], jnp.logical_and(u < NB[rho], (u & 1) == core)))
            def _(rho=rho):
                own(rho, u)

            late = u - 2
            odd = jnp.logical_and(core == 0, (late & 1) == 1)

            @pl.when(jnp.logical_and(jnp.logical_and(is_root[rho], odd), jnp.logical_and(late >= 0, late < NB[rho])))
            def _(rho=rho, late=late):
                own_other(rho, late)

        for act in (forward, share):
            for rho in range(2):
                for il in range(2):
                    n = u - LAG * depth[rho][il]
                    theirs = jnp.logical_not(is_root[rho])

                    @pl.when(jnp.logical_and(jnp.logical_and(n >= 0, n < NB[rho]), theirs))
                    def _(act=act, rho=rho, il=il, n=n):
                        act(rho, il, n)

        for rho in range(2):
            for il in range(2):
                n = u - LAG * depth[rho][il] - x_lag

                @pl.when(jnp.logical_and(n >= 0, n < NB[rho]))
                def _(rho=rho, il=il, n=n):
                    x_arrive(rho, il, n)

        @pl.when(u == 0)
        def _():
            load_f.wait()

        @pl.when(u < 16)
        def _():
            rows = pl.ds(pl.multiple_of(u * 64, 64), 64)
            hi, lo = split(fv[rows, :])
            fh[rows, :] = hi
            fl[rows, :] = lo

        for n in range(NL[1]):

            @pl.when(u == WAIT + n)
            def _(n=n):
                take_g(n)

        @pl.when(u == WAIT)
        def _():
            load_c.wait()

        g = u - WAIT - START

        @pl.when(jnp.logical_and(g >= 0, g < 8))
        def _():
            q = g >> 1

            @pl.when((g & 1) == 0)
            def _():
                solve_group(q)
                update_group(q, 0)

            @pl.when((g & 1) == 1)
            def _():
                update_group(q, 1)

        return carry

    lax.fori_loop(0, UNITS, step, 0)

    @pl.when(p == 0)
    def _():
        for s in range(4):
            xb[s] = w[b_index(qz, s), :, lanes]

    @pl.when(p != 0)
    def _():
        for s in range(4):
            for il in range(2):
                ref = x_piece(s, 2 * (1 - core) + il)
                remote(ref, ref, xss.at[s, il], xsb.at[s, il], sibling).wait_recv()

    parts = [split(xb[s]) for s in range(2)]
    hi, lo = (jnp.concatenate([parts[0][i], parts[1][i]], axis=0) for i in range(2))
    for s, v in enumerate([xb[0], xb[1], *finish(xb[2], xb[3], hi, lo)]):
        sbt[:, pl.ds(s * B, B)] = v.T
    load_p.wait()
    sh, sl = split(sbt[pl.ds(pl.multiple_of(core * 64, 64), 64), :])

    for q in range(4):
        cols = pl.ds(q * B, B)
        tv[:, cols] = pv[:, cols] - dot3(sh, sl, xh[:, cols], xl[:, cols])

    save_p = pltpu.make_async_copy(tv, post_hbm, out_sem.at[4])
    save_p.start()

    for rho in range(2):
        whole = w.at[pl.ds(0, NB[rho]), pl.ds(0, PIECE)]

        @pl.when(is_root[rho])
        def _(rho=rho):
            own_wait(0)
            own_wait(1)
            for j in range(NB[rho] // 2):
                whole_copy(0, 2 * j).wait_send()

        @pl.when(jnp.logical_not(is_root[rho]))
        def _(rho=rho, whole=whole):
            for il in range(2):
                for d in range(4):

                    @pl.when(((child[rho][il] >> d) & 1) == 1)
                    def _(il=il, d=d):
                        remote(whole, whole, child_sem.at[rho, il, d], rs.at[0, il], near_same[d]).wait_send()

                remote(whole, whole, sib_sem.at[rho, il], rs.at[0, il], sibling).wait_send()

    def x_sent(i, s, il):
        ref = x_piece(s, 2 * core + il)
        remote(ref, ref, xs.at[i, s, il], xr.at[s, il], sibling).wait_send()

    for s in range(4):
        for il in range(2):

            @pl.when(p == 0)
            def _(s=s, il=il):
                x_sent(0, s, il)
                x_sent(1, s, il)

            @pl.when(relays)
            def _(s=s, il=il):
                x_sent(0, s, il)

            @pl.when(p != 0)
            def _(s=s, il=il):
                ref = x_piece(s, 2 * core + il)
                remote(ref, ref, xss.at[s, il], xsb.at[s, il], sibling).wait_send()

    save_p.wait()
    for q in range(4):
        cols = pl.ds(q * B, B)
        pltpu.make_async_copy(cv.at[:, cols], out_hbm.at[:, cols], out_sem.at[q]).wait()


def local(cross_cov, factor_cols, prior_cov):
    n = 1024
    dma = pltpu.SemaphoreType.DMA
    any_space = pl.BlockSpec(memory_space=pl.ANY)
    return pl.pallas_call(
        kernel,
        out_shape=(jax.ShapeDtypeStruct((n, n), F32), jax.ShapeDtypeStruct((64, n), F32)),
        in_specs=[any_space] * 3,
        out_specs=(any_space, any_space),
        scratch_shapes=[
            pltpu.VMEM((BLOCKS, B, B), F32),
            pltpu.VMEM((n, n), F32),
            pltpu.VMEM((n, n), BF16),
            pltpu.VMEM((n, n), BF16),
            pltpu.VMEM((n, n), F32),
            pltpu.VMEM((64, n), F32),
            pltpu.VMEM((n, n), BF16),
            pltpu.VMEM((n, n), BF16),
            pltpu.VMEM((2 * B, 2 * B), BF16),
            pltpu.VMEM((2 * B, 2 * B), BF16),
            pltpu.VMEM((4, B, B), BF16),
            pltpu.VMEM((B, B), F32),
            pltpu.VMEM((B, B), F32),
            pltpu.VMEM((4, B, 128), F32),
            pltpu.VMEM((128, n), F32),
            pltpu.VMEM((64, n), F32),
            dma((BLOCKS, 2)),
            dma((BLOCKS, 2)),
            dma((2, 2, 4)),
            dma((2, 2)),
            dma((2, 4)),
            dma((6,)),
            dma((6,)),
            dma((3,)),
            dma((8,)),
            dma((5,)),
            dma((4, 2)),
            dma((2, 4, 2)),
            dma((4, 2)),
            dma((4, 2)),
        ],
        compiler_params=pltpu.CompilerParams(
            collective_id=0, has_side_effects=True, vmem_limit_bytes=56 * 1024 * 1024
        ),
        name="solve_update",
    )(cross_cov, factor_cols, prior_cov)


def solution(mesh):
    placed = (P("row", "cand"), P("row", None), P("row", "cand"))
    return jax.shard_map(
        local,
        mesh=mesh,
        in_specs=placed,
        out_specs=(P("row", "cand"), P("row", "cand")),
        check_vma=False,
    )
```

```python
import functools

import jax
import jax.numpy as jnp
from jax import lax
from jax.experimental import pallas as pl
from jax.experimental.pallas import tpu as pltpu
from jax.sharding import PartitionSpec as P

MESH = pl.DeviceIdType.MESH
F32, BF16 = jnp.float32, jnp.bfloat16
HIGHEST = lax.Precision.HIGHEST
B = 256
PIECE = 64
LAG = 2

TREES = (
    (2, 112, 98, 82, 74, 62, 46, 22, 48, 96, 112, 98, 86, 66, 48, 37, 65, 93, 96, 112, 98, 81, 96, 49, 80, 96, 112, 98, 82, 72, 49, 65),
    (1, 21, 45, 61, 69, 81, 97, 112, 48, 38, 48, 64, 81, 97, 112, 96, 66, 50, 96, 82, 97, 112, 96, 94, 80, 66, 50, 73, 89, 97, 112, 96),
    (8, 48, 64, 80, 96, 80, 64, 48, 48, 96, 82, 96, 112, 96, 81, 96, 40, 48, 73, 88, 104, 90, 74, 48, 27, 45, 61, 68, 84, 70, 62, 46),
    (4, 56, 64, 80, 96, 80, 64, 56, 23, 41, 61, 77, 88, 76, 62, 42, 36, 80, 70, 85, 100, 84, 69, 80, 48, 64, 80, 96, 112, 96, 80, 64),
)
STEP = ((0, 1), (0, 7), (1, 0), (3, 0))
FIRST = (1, 0, 3, 2)
NL = (0, 4)
NB = (8, 12)
BASE = (0, 8)
BLOCKS = 20
WAIT = LAG * 7
STEPS = (8, 10)
UNITS = STEPS[1] + WAIT + 4


def b_index(q, s):
    return BASE[s // 2] + NL[s // 2] + 2 * q + s % 2


def split(x):
    hi = x.astype(BF16)
    return hi, (x - hi.astype(F32)).astype(BF16)


def dot(a, b):
    return jnp.dot(a, b, preferred_element_type=F32)


def dot3(ah, al, bh, bl):
    return dot(ah, bh) + (dot(ah, bl) + dot(al, bh))


def dotf(a, b):
    return jnp.dot(a, b, precision=HIGHEST, preferred_element_type=F32)


def invert_block(d):
    n = d.shape[0]
    ri = lax.broadcasted_iota(jnp.int32, (n, n), 0)
    ci = lax.broadcasted_iota(jnp.int32, (n, n), 1)
    same = ri == ci
    on_diag = jnp.where(same, d, 0.0)
    by_row = 1.0 / jnp.sum(on_diag, axis=1, keepdims=True)
    by_col = 1.0 / jnp.sum(on_diag, axis=0, keepdims=True)
    low = jnp.where(ri > ci, d, 0.0) * by_row
    inv = jnp.where(same, 1.0, 0.0) - jnp.where((ri >> 1) == (ci >> 1), low, 0.0)
    k = 1
    while 2 << k <= n:
        off = jnp.where(((ri >> (k + 1)) == (ci >> (k + 1))) & ((ri >> k) != (ci >> k)), low, 0.0)
        inv = inv - dotf(dotf(inv, off), inv)
        k += 1
    return inv * by_col


def invert_lower(d):
    h = B // 2
    first, last = invert_block(d[:h, :h]), invert_block(d[h:, h:])
    corner = -dotf(dotf(last, d[h:, :h]), first)
    top = jnp.concatenate([first, jnp.zeros((h, h), F32)], axis=1)
    return jnp.concatenate([top, jnp.concatenate([corner, last], axis=1)], axis=0)


def kernel(
    c_hbm, f_hbm, p_hbm, cv, tv,
    w, fv, fh, fl, pv, xh, xl, gh, gl, dsp, dv, lv, xb, sbt,
    rs, sb, child_sem, sib_sem, own_sem, pre_s, pre_r, load_sem, raw_sem, xr, xs, xsb, xss,
):
    row = lax.axis_index("row")
    x = lax.axis_index("cand")
    y = row >> 4
    z = (row >> 1) & 7
    core = row & 1

    def device(yy, zz, cc, xx=None):
        return ((yy & 3) * 16 + (zz & 7) * 2 + cc, x if xx is None else xx & 3)

    sibling = device(y, z, 1 - core)
    near = [[device(y + dy, z + dz, cc) for cc in range(2)] for dy, dz in STEP]
    near_same = [device(y + dy, z + dz, core) for dy, dz in STEP]
    beside = [device(y, z, core, x + dx) for dx in (1, 3)]

    def remote(src, dst, send_sem, recv_sem, to):
        return pltpu.make_async_remote_copy(
            src_ref=src, dst_ref=dst, send_sem=send_sem, recv_sem=recv_sem, device_id=to, device_id_type=MESH
        )

    load_f = pltpu.make_async_copy(f_hbm, fv, load_sem.at[0])
    load_c = pltpu.make_async_copy(c_hbm, cv, load_sem.at[1])
    load_p = pltpu.make_async_copy(p_hbm, pv, load_sem.at[2])

    def raw_copies(s):
        found = [(w.at[b_index(q, s)], c_hbm.at[pl.ds(0, B), pl.ds(q * B, B)]) for q in range(4)]
        for t in range(2 if s >= 2 else 0):
            found.append((w.at[BASE[1] + 2 * t + s % 2], f_hbm.at[pl.ds(0, B), pl.ds(t * B, B)]))
        if s % 2:
            found.append((lv, f_hbm.at[pl.ds(0, B), pl.ds((s - 1) * B, B)]))
        return [pltpu.make_async_copy(src, dst, raw_sem.at[i]) for i, (dst, src) in enumerate(found)]

    def load_d(s):
        return pltpu.make_async_copy(f_hbm.at[pl.ds(0, B), pl.ds(s * B, B)], dv, raw_sem.at[7])

    for s in range(4):

        @pl.when(row == s)
        def _(s=s):
            load_d(s).start()
            for c in raw_copies(s):
                c.start()

    barrier = pltpu.get_barrier_semaphore()
    for to in [t for pair in near for t in pair] + beside + [sibling]:
        pl.semaphore_signal(barrier, inc=1, device_id=to, device_id_type=MESH)
    load_f.start()
    load_c.start()
    load_p.start()

    for s in range(4):

        @pl.when(row == s)
        def _(s=s):
            load_d(s).wait()
            dsp[0], dsp[1] = split(invert_lower(dv[...]))
            for c in raw_copies(s):
                c.wait()
            if s % 2:
                dsp[2], dsp[3] = split(lv[...])

    def lookup(table, key):
        found = jnp.int32(0)
        for k, v in enumerate(table):
            found = jnp.where(key == k, v, found)
        return found

    is_root, depth, child = [], [], []
    for rho in range(2):
        idx = y * 8 + ((z - rho) & 7)
        merged = [TREES[2 * cc][k] + 128 * TREES[2 * cc + 1][k] for cc in range(2) for k in range(32)]
        v = lookup(merged, core * 32 + idx)
        is_root.append(idx == 0)
        depth.append(((v >> 4) & 7, v >> 11))
        child.append((v & 15, (v >> 7) & 15))

    p = (x - y) & 3
    qz = z >> 1
    lanes = pl.ds(pl.multiple_of((z & 1) * 128, 128), 128)
    relays = jnp.logical_or(jnp.logical_and(p == 1, core == 0), jnp.logical_and(p == 3, core == 1))
    onward = (beside[0][0], (x + jnp.where(core == 0, 1, 3)) & 3)
    x_lag = jnp.where(p == 2, 4, 2)

    pl.semaphore_wait(barrier, 11)

    def piece(b, tree):
        return w.at[b, pl.ds(pl.multiple_of(tree * 64, 64), PIECE)]

    def x_piece(s, tree):
        return xb.at[s, pl.ds(pl.multiple_of(tree * 64, 64), PIECE)]

    def needed(rho, n):
        m = n - NL[rho]
        return jnp.logical_and(m >= 0, (m >> 1) == qz), 2 * rho + (m & 1)

    def x_start(rho, il, n):
        hit, s = needed(rho, n)

        @pl.when(jnp.logical_and(p == 0, hit))
        def _():
            tree = 2 * core + il
            src = w.at[BASE[rho] + n, pl.ds(pl.multiple_of(tree * 64, 64), PIECE), lanes]
            for i in range(2):
                remote(src, x_piece(s, tree), xs.at[i, s, il], xr.at[s, il], beside[i]).start()

    def x_arrive(rho, il, n):
        hit, s = needed(rho, n)

        @pl.when(jnp.logical_and(p != 0, hit))
        def _():
            ref = x_piece(s, 2 * core + il)
            remote(ref, ref, xs.at[0, s, il], xr.at[s, il], sibling).wait_recv()

            @pl.when(relays)
            def _():
                remote(ref, ref, xs.at[0, s, il], xr.at[s, il], onward).start()

            remote(ref, ref, xss.at[s, il], xsb.at[s, il], sibling).start()

    def whole_copy(b, n):
        ref = w.at[b]
        return remote(ref, ref, pre_s.at[n >> 1], pre_r.at[n >> 1], sibling)

    def own_sends(b, slot):
        for tree in range(4):
            ref = w.at[b, pl.ds(64 * tree, PIECE)]
            yield remote(ref, ref, own_sem.at[slot, tree], rs.at[b, tree % 2], near[FIRST[tree]][tree // 2])

    def own_wait(slot):
        for copy in own_sends(0, slot):
            copy.wait_send()

    def own(rho, n):
        b = BASE[rho] + n
        j = n >> 1
        slot = j & 1

        @pl.when(core == 1)
        def _():
            whole_copy(b - 1, n).wait_recv()
            for il in range(2):
                x_start(rho, il, n - 1)
            w[b] = w[b] - dot3(dsp[2], dsp[3], *split(w[b - 1]))

        w[b] = dot3(dsp[0], dsp[1], *split(w[b]))
        whole_copy(b, n).start()

        @pl.when(j >= 2)
        def _():
            own_wait(slot)

        for copy in own_sends(b, slot):
            copy.start()
        for il in range(2):
            x_start(rho, il, n)

    def own_other(rho, n):
        whole_copy(BASE[rho] + n, n).wait_recv()
        for il in range(2):
            x_start(rho, il, n)

    def forward(rho, il, n):
        b = BASE[rho] + n
        ref = piece(b, 2 * core + il)
        remote(ref, ref, sib_sem.at[rho, il], rs.at[b, il], sibling).wait_recv()
        for d in range(4):

            @pl.when(((child[rho][il] >> d) & 1) == 1)
            def _(d=d):
                remote(ref, ref, child_sem.at[rho, il, d], rs.at[b, il], near_same[d]).start()

    def share(rho, il, n):
        b = BASE[rho] + n
        ref = piece(b, 2 * core + il)
        remote(ref, ref, sib_sem.at[rho, il], sb.at[b, il], sibling).start()
        x_start(rho, il, n)

    def wait_other(rho, n):
        b = BASE[rho] + n

        @pl.when(jnp.logical_not(is_root[rho]))
        def _():
            for il in range(2):
                ref = piece(b, 2 * (1 - core) + il)
                remote(ref, ref, sib_sem.at[rho, il], sb.at[b, il], sibling).wait_recv()

    def take_g(n):
        wait_other(1, n)
        half, t = n % 2, n // 2
        rows, cols = pl.ds(half * B, B), pl.ds(t * B, B)
        gh[rows, cols], gl[rows, cols] = split(w[BASE[1] + n])

    def finish(y2, y3, hi, lo):
        r = dot3(gh[...], gl[...], hi, lo)
        return y2 - r[:B], y3 - r[B:]

    def columns(q):
        return pl.ds(pl.multiple_of(q * B, B), B)

    def update(q, half):
        cols = columns(q)
        depth_part = pl.ds(half * 2 * B, 2 * B)
        for m in range(4):
            rows = pl.ds(m * B, B)
            cv[rows, cols] = cv[rows, cols] - dot3(
                fh[rows, depth_part], fl[rows, depth_part], xh[depth_part, cols], xl[depth_part, cols]
            )

    def first_half(q):
        cols = columns(q)
        for s in range(2):
            wait_other(0, 2 * q + s)
            xh[pl.ds(s * B, B), cols], xl[pl.ds(s * B, B), cols] = split(w[b_index(q, s)])
        update(q, 0)

    def second_half(q):
        cols = columns(q)
        for s in range(2, 4):
            wait_other(1, b_index(q, s) - BASE[1])
        top = pl.ds(0, 2 * B)
        last = finish(w[b_index(q, 2)], w[b_index(q, 3)], xh[top, cols], xl[top, cols])
        for s in range(2, 4):
            xh[pl.ds(s * B, B), cols], xl[pl.ds(s * B, B), cols] = split(last[s - 2])
        update(q, 1)
        for s in range(4):

            @pl.when(row == s)
            def _(s=s):
                cv[pl.ds(0, B), cols] = w[b_index(q, s)] if s < 2 else last[s - 2]

    def step(u, carry):
        def blocks_at(rho, v):
            inside = jnp.logical_and(v >= 0, v < STEPS[rho])
            if rho == 0:
                return [(inside, v)]
            early = jnp.logical_and(v >= 0, v < 2)
            return [(inside, jnp.where(early, 2 * v, v + 2)), (early, 2 * v + 1)]

        for rho in range(2):
            for inside, n in blocks_at(rho, u):

                @pl.when(jnp.logical_and(is_root[rho], jnp.logical_and(inside, (n & 1) == core)))
                def _(rho=rho, n=n):
                    own(rho, n)

            for inside, n in blocks_at(rho, u - 2):
                odd = jnp.logical_and(core == 0, (n & 1) == 1)

                @pl.when(jnp.logical_and(is_root[rho], jnp.logical_and(inside, odd)))
                def _(rho=rho, n=n):
                    own_other(rho, n)

        for act in (forward, share):
            for rho in range(2):
                for il in range(2):
                    for inside, n in blocks_at(rho, u - LAG * depth[rho][il]):

                        @pl.when(jnp.logical_and(inside, jnp.logical_not(is_root[rho])))
                        def _(act=act, rho=rho, il=il, n=n):
                            act(rho, il, n)

        for rho in range(2):
            for il in range(2):
                inside, n = blocks_at(rho, u - LAG * depth[rho][il] - x_lag)[0]

                @pl.when(inside)
                def _(rho=rho, il=il, n=n):
                    x_arrive(rho, il, n)

        @pl.when(u == 0)
        def _():
            load_f.wait()

        @pl.when(u < 16)
        def _():
            rows = pl.ds(pl.multiple_of(u * 64, 64), 64)
            hi, lo = split(fv[rows, :])
            fh[rows, :] = hi
            fl[rows, :] = lo

        for n in range(NL[1]):

            @pl.when(u == WAIT + n // 2)
            def _(n=n):
                take_g(n)

        @pl.when(u == WAIT)
        def _():
            load_c.wait()

        g = u - WAIT

        @pl.when(jnp.logical_and((g & 1) == 1, jnp.logical_and(g >= 1, g < 8)))
        def _():
            first_half(g >> 1)

        second = jnp.logical_and((g & 1) == 0, jnp.logical_and(g >= 4, g < 9))

        @pl.when(jnp.logical_or(second, g == 9))
        def _():
            second_half((g - 3) >> 1)

        return carry

    lax.fori_loop(0, UNITS, step, 0)

    @pl.when(p == 0)
    def _():
        for s in range(4):
            xb[s] = w[b_index(qz, s), :, lanes]

    @pl.when(p != 0)
    def _():
        for s in range(4):
            for il in range(2):
                ref = x_piece(s, 2 * (1 - core) + il)
                remote(ref, ref, xss.at[s, il], xsb.at[s, il], sibling).wait_recv()

    parts = [split(xb[s]) for s in range(2)]
    hi, lo = (jnp.concatenate([parts[0][i], parts[1][i]], axis=0) for i in range(2))
    for s, v in enumerate([xb[0], xb[1], *finish(xb[2], xb[3], hi, lo)]):
        sbt[:, pl.ds(s * B, B)] = v.T
    load_p.wait()
    sh, sl = split(sbt[pl.ds(pl.multiple_of(core * 64, 64), 64), :])

    for q in range(4):
        cols = pl.ds(q * B, B)
        tv[:, cols] = pv[:, cols] - dot3(sh, sl, xh[:, cols], xl[:, cols])

    for rho in range(2):
        whole = w.at[pl.ds(0, NB[rho]), pl.ds(0, PIECE)]

        @pl.when(is_root[rho])
        def _(rho=rho):
            own_wait(0)
            own_wait(1)
            for j in range(NB[rho] // 2):
                whole_copy(0, 2 * j).wait_send()

        @pl.when(jnp.logical_not(is_root[rho]))
        def _(rho=rho, whole=whole):
            for il in range(2):
                for d in range(4):

                    @pl.when(((child[rho][il] >> d) & 1) == 1)
                    def _(il=il, d=d):
                        remote(whole, whole, child_sem.at[rho, il, d], rs.at[0, il], near_same[d]).wait_send()

                remote(whole, whole, sib_sem.at[rho, il], rs.at[0, il], sibling).wait_send()

    def x_sent(i, s, il):
        ref = x_piece(s, 2 * core + il)
        remote(ref, ref, xs.at[i, s, il], xr.at[s, il], sibling).wait_send()

    for s in range(4):
        for il in range(2):

            @pl.when(p == 0)
            def _(s=s, il=il):
                x_sent(0, s, il)
                x_sent(1, s, il)

            @pl.when(relays)
            def _(s=s, il=il):
                x_sent(0, s, il)

            @pl.when(p != 0)
            def _(s=s, il=il):
                ref = x_piece(s, 2 * core + il)
                remote(ref, ref, xss.at[s, il], xsb.at[s, il], sibling).wait_send()


def local(cross_cov, factor_cols, prior_cov):
    n = 1024
    dma = pltpu.SemaphoreType.DMA
    in_hbm = pl.BlockSpec(memory_space=pltpu.HBM)
    current, posterior = pl.pallas_call(
        kernel,
        out_shape=(pltpu.VMEM((n, n), F32), pltpu.VMEM((64, n), F32)),
        in_specs=[in_hbm] * 3,
        out_specs=(pl.BlockSpec(memory_space=pltpu.VMEM),) * 2,
        scratch_shapes=[
            pltpu.VMEM((BLOCKS, B, B), F32),
            pltpu.VMEM((n, n), F32),
            pltpu.VMEM((n, n), BF16),
            pltpu.VMEM((n, n), BF16),
            pltpu.VMEM((64, n), F32),
            pltpu.VMEM((n, n), BF16),
            pltpu.VMEM((n, n), BF16),
            pltpu.VMEM((2 * B, 2 * B), BF16),
            pltpu.VMEM((2 * B, 2 * B), BF16),
            pltpu.VMEM((4, B, B), BF16),
            pltpu.VMEM((B, B), F32),
            pltpu.VMEM((B, B), F32),
            pltpu.VMEM((4, B, 128), F32),
            pltpu.VMEM((128, n), F32),
            dma((BLOCKS, 2)),
            dma((BLOCKS, 2)),
            dma((2, 2, 4)),
            dma((2, 2)),
            dma((2, 4)),
            dma((6,)),
            dma((6,)),
            dma((3,)),
            dma((8,)),
            dma((4, 2)),
            dma((2, 4, 2)),
            dma((4, 2)),
            dma((4, 2)),
        ],
        compiler_params=pltpu.CompilerParams(
            collective_id=0, has_side_effects=True, vmem_limit_bytes=int(59.5 * 1024 * 1024)
        ),
        name="solve_update",
    )(cross_cov, factor_cols, prior_cov)
    return hand_on(current, posterior)


def hand_on_kernel(a_in, b_in, a_out, b_out, sem):
    rows = 256
    copies = [
        pltpu.make_async_copy(a_in.at[pl.ds(i * rows, rows)], a_out.at[pl.ds(i * rows, rows)], sem.at[i])
        for i in range(4)
    ]
    copies.append(pltpu.make_async_copy(b_in, b_out, sem.at[4]))
    for c in copies:
        c.start()
    for c in copies:
        c.wait()


def hand_on(current, posterior):
    return pl.pallas_call(
        hand_on_kernel,
        out_shape=(jax.ShapeDtypeStruct(current.shape, F32), jax.ShapeDtypeStruct(posterior.shape, F32)),
        in_specs=[pl.BlockSpec(memory_space=pltpu.VMEM)] * 2,
        out_specs=(pl.BlockSpec(memory_space=pltpu.HBM),) * 2,
        scratch_shapes=[pltpu.SemaphoreType.DMA((5,))],
        name="hand_on",
    )(current, posterior)


def solution(mesh):
    placed = (P("row", "cand"), P("row", None), P("row", "cand"))
    return jax.shard_map(
        local,
        mesh=mesh,
        in_specs=placed,
        out_specs=(P("row", "cand"), P("row", "cand")),
        check_vma=False,
    )
```

```python
import functools

import jax
import jax.numpy as jnp
from jax import lax
from jax.experimental import pallas as pl
from jax.experimental.pallas import tpu as pltpu
from jax.sharding import PartitionSpec as P

MESH = pl.DeviceIdType.MESH
F32, BF16 = jnp.float32, jnp.bfloat16
HIGHEST = lax.Precision.HIGHEST
B = 256
PIECE = 64
LAG = 2

TREES = (
    (2, 112, 98, 82, 74, 62, 46, 22, 48, 96, 112, 98, 86, 66, 48, 37, 65, 93, 96, 112, 98, 81, 96, 49, 80, 96, 112, 98, 82, 72, 49, 65),
    (1, 21, 45, 61, 69, 81, 97, 112, 48, 38, 48, 64, 81, 97, 112, 96, 66, 50, 96, 82, 97, 112, 96, 94, 80, 66, 50, 73, 89, 97, 112, 96),
    (8, 48, 64, 80, 96, 80, 64, 48, 48, 96, 82, 96, 112, 96, 81, 96, 40, 48, 73, 88, 104, 90, 74, 48, 27, 45, 61, 68, 84, 70, 62, 46),
    (4, 56, 64, 80, 96, 80, 64, 56, 23, 41, 61, 77, 88, 76, 62, 42, 36, 80, 70, 85, 100, 84, 69, 80, 48, 64, 80, 96, 112, 96, 80, 64),
)
STEP = ((0, 1), (0, 7), (1, 0), (3, 0))
FIRST = (1, 0, 3, 2)
NL = (0, 4)
NB = (8, 12)
BASE = (0, 8)
BLOCKS = 20
WAIT = LAG * 7
STEPS = (8, 10)
UNITS = STEPS[1] + WAIT + 4


def b_index(q, s):
    return BASE[s // 2] + NL[s // 2] + 2 * q + s % 2


def split(x):
    hi = x.astype(BF16)
    return hi, (x - hi.astype(F32)).astype(BF16)


def dot(a, b):
    return jnp.dot(a, b, preferred_element_type=F32)


def dot3(ah, al, bh, bl):
    return dot(ah, bh) + (dot(ah, bl) + dot(al, bh))


def dotf(a, b):
    return jnp.dot(a, b, precision=HIGHEST, preferred_element_type=F32)


def invert_block(d):
    n = d.shape[0]
    ri = lax.broadcasted_iota(jnp.int32, (n, n), 0)
    ci = lax.broadcasted_iota(jnp.int32, (n, n), 1)
    same = ri == ci
    on_diag = jnp.where(same, d, 0.0)
    by_row = 1.0 / jnp.sum(on_diag, axis=1, keepdims=True)
    by_col = 1.0 / jnp.sum(on_diag, axis=0, keepdims=True)
    low = jnp.where(ri > ci, d, 0.0) * by_row
    inv = jnp.where(same, 1.0, 0.0) - jnp.where((ri >> 1) == (ci >> 1), low, 0.0)
    k = 1
    while 2 << k <= n:
        off = jnp.where(((ri >> (k + 1)) == (ci >> (k + 1))) & ((ri >> k) != (ci >> k)), low, 0.0)
        inv = inv - dotf(dotf(inv, off), inv)
        k += 1
    return inv * by_col


def invert_lower(d):
    h = B // 2
    first, last = invert_block(d[:h, :h]), invert_block(d[h:, h:])
    corner = -dotf(dotf(last, d[h:, :h]), first)
    top = jnp.concatenate([first, jnp.zeros((h, h), F32)], axis=1)
    return jnp.concatenate([top, jnp.concatenate([corner, last], axis=1)], axis=0)


def kernel(
    c_hbm, f_hbm, p_hbm, cv, tv,
    w, fv, fh, fl, pv, xh, xl, gh, gl, dsp, dv, lv, xb, sbt,
    rs, sb, child_sem, sib_sem, own_sem, pre_s, pre_r, load_sem, raw_sem, xr, xs, xsb, xss,
):
    row = lax.axis_index("row")
    x = lax.axis_index("cand")
    y = row >> 4
    z = (row >> 1) & 7
    core = row & 1

    def device(yy, zz, cc, xx=None):
        return ((yy & 3) * 16 + (zz & 7) * 2 + cc, x if xx is None else xx & 3)

    sibling = device(y, z, 1 - core)
    near = [[device(y + dy, z + dz, cc) for cc in range(2)] for dy, dz in STEP]
    near_same = [device(y + dy, z + dz, core) for dy, dz in STEP]
    beside = [device(y, z, core, x + dx) for dx in (1, 3)]

    def remote(src, dst, send_sem, recv_sem, to):
        return pltpu.make_async_remote_copy(
            src_ref=src, dst_ref=dst, send_sem=send_sem, recv_sem=recv_sem, device_id=to, device_id_type=MESH
        )

    load_f = pltpu.make_async_copy(f_hbm, fv, load_sem.at[0])
    load_c = pltpu.make_async_copy(c_hbm, cv, load_sem.at[1])
    load_p = pltpu.make_async_copy(p_hbm, pv, load_sem.at[2])

    def raw_copies(s):
        found = [(w.at[b_index(q, s)], c_hbm.at[pl.ds(0, B), pl.ds(q * B, B)]) for q in range(4)]
        for t in range(2 if s >= 2 else 0):
            found.append((w.at[BASE[1] + 2 * t + s % 2], f_hbm.at[pl.ds(0, B), pl.ds(t * B, B)]))
        if s % 2:
            found.append((lv, f_hbm.at[pl.ds(0, B), pl.ds((s - 1) * B, B)]))
        return [pltpu.make_async_copy(src, dst, raw_sem.at[i]) for i, (dst, src) in enumerate(found)]

    def load_d(s):
        return pltpu.make_async_copy(f_hbm.at[pl.ds(0, B), pl.ds(s * B, B)], dv, raw_sem.at[7])

    for s in range(4):

        @pl.when(row == s)
        def _(s=s):
            load_d(s).start()
            for c in raw_copies(s):
                c.start()

    barrier = pltpu.get_barrier_semaphore()
    for to in [t for pair in near for t in pair] + beside + [sibling]:
        pl.semaphore_signal(barrier, inc=1, device_id=to, device_id_type=MESH)
    load_f.start()
    load_c.start()
    load_p.start()

    for s in range(4):

        @pl.when(row == s)
        def _(s=s):
            load_d(s).wait()
            dsp[0], dsp[1] = split(invert_lower(dv[...]))
            for c in raw_copies(s):
                c.wait()
            if s % 2:
                dsp[2], dsp[3] = split(lv[...])

    def lookup(table, key):
        found = jnp.int32(0)
        for k, v in enumerate(table):
            found = jnp.where(key == k, v, found)
        return found

    is_root, depth, child = [], [], []
    for rho in range(2):
        idx = y * 8 + ((z - rho) & 7)
        merged = [TREES[2 * cc][k] + 128 * TREES[2 * cc + 1][k] for cc in range(2) for k in range(32)]
        v = lookup(merged, core * 32 + idx)
        is_root.append(idx == 0)
        depth.append(((v >> 4) & 7, v >> 11))
        child.append((v & 15, (v >> 7) & 15))

    p = (x - y) & 3
    qz = z >> 1
    lanes = pl.ds(pl.multiple_of((z & 1) * 128, 128), 128)
    relays = jnp.logical_or(jnp.logical_and(p == 1, core == 0), jnp.logical_and(p == 3, core == 1))
    onward = (beside[0][0], (x + jnp.where(core == 0, 1, 3)) & 3)
    x_lag = jnp.where(p == 2, 4, 2)

    pl.semaphore_wait(barrier, 11)

    def piece(b, tree):
        return w.at[b, pl.ds(pl.multiple_of(tree * 64, 64), PIECE)]

    def x_piece(s, tree):
        return xb.at[s, pl.ds(pl.multiple_of(tree * 64, 64), PIECE)]

    def needed(rho, n):
        m = n - NL[rho]
        return jnp.logical_and(m >= 0, (m >> 1) == qz), 2 * rho + (m & 1)

    def x_start(rho, il, n):
        hit, s = needed(rho, n)

        @pl.when(jnp.logical_and(p == 0, hit))
        def _():
            tree = 2 * core + il
            src = w.at[BASE[rho] + n, pl.ds(pl.multiple_of(tree * 64, 64), PIECE), lanes]
            for i in range(2):
                remote(src, x_piece(s, tree), xs.at[i, s, il], xr.at[s, il], beside[i]).start()

    def x_arrive(rho, il, n):
        hit, s = needed(rho, n)

        @pl.when(jnp.logical_and(p != 0, hit))
        def _():
            ref = x_piece(s, 2 * core + il)
            remote(ref, ref, xs.at[0, s, il], xr.at[s, il], sibling).wait_recv()

            @pl.when(relays)
            def _():
                remote(ref, ref, xs.at[0, s, il], xr.at[s, il], onward).start()

            remote(ref, ref, xss.at[s, il], xsb.at[s, il], sibling).start()

    def whole_copy(b, n):
        ref = w.at[b]
        return remote(ref, ref, pre_s.at[n >> 1], pre_r.at[n >> 1], sibling)

    def own_sends(b, slot):
        for tree in range(4):
            ref = w.at[b, pl.ds(64 * tree, PIECE)]
            yield remote(ref, ref, own_sem.at[slot, tree], rs.at[b, tree % 2], near[FIRST[tree]][tree // 2])

    def own_wait(slot):
        for copy in own_sends(0, slot):
            copy.wait_send()

    def own(rho, n):
        b = BASE[rho] + n
        j = n >> 1
        slot = j & 1

        @pl.when(core == 1)
        def _():
            whole_copy(b - 1, n).wait_recv()
            for il in range(2):
                x_start(rho, il, n - 1)
            w[b] = w[b] - dot3(dsp[2], dsp[3], *split(w[b - 1]))

        w[b] = dot3(dsp[0], dsp[1], *split(w[b]))
        whole_copy(b, n).start()

        @pl.when(j >= 2)
        def _():
            own_wait(slot)

        for copy in own_sends(b, slot):
            copy.start()
        for il in range(2):
            x_start(rho, il, n)

    def own_other(rho, n):
        whole_copy(BASE[rho] + n, n).wait_recv()
        for il in range(2):
            x_start(rho, il, n)

    def forward(rho, il, n):
        b = BASE[rho] + n
        ref = piece(b, 2 * core + il)
        remote(ref, ref, sib_sem.at[rho, il], rs.at[b, il], sibling).wait_recv()
        for d in range(4):

            @pl.when(((child[rho][il] >> d) & 1) == 1)
            def _(d=d):
                remote(ref, ref, child_sem.at[rho, il, d], rs.at[b, il], near_same[d]).start()

    def share(rho, il, n):
        b = BASE[rho] + n
        ref = piece(b, 2 * core + il)
        remote(ref, ref, sib_sem.at[rho, il], sb.at[b, il], sibling).start()
        x_start(rho, il, n)

    def wait_other(rho, n):
        b = BASE[rho] + n

        @pl.when(jnp.logical_not(is_root[rho]))
        def _():
            for il in range(2):
                ref = piece(b, 2 * (1 - core) + il)
                remote(ref, ref, sib_sem.at[rho, il], sb.at[b, il], sibling).wait_recv()

    def take_g(n):
        wait_other(1, n)
        half, t = n % 2, n // 2
        rows, cols = pl.ds(half * B, B), pl.ds(t * B, B)
        gh[rows, cols], gl[rows, cols] = split(w[BASE[1] + n])

    def finish(y2, y3, hi, lo):
        r = dot3(gh[...], gl[...], hi, lo)
        return y2 - r[:B], y3 - r[B:]

    def columns(q):
        return pl.ds(pl.multiple_of(q * B, B), B)

    def update(q, half):
        cols = columns(q)
        depth_part = pl.ds(half * 2 * B, 2 * B)
        for m in range(4):
            rows = pl.ds(m * B, B)
            cv[rows, cols] = cv[rows, cols] - dot3(
                fh[rows, depth_part], fl[rows, depth_part], xh[depth_part, cols], xl[depth_part, cols]
            )

    def first_half(q):
        cols = columns(q)
        for s in range(2):
            wait_other(0, 2 * q + s)
            xh[pl.ds(s * B, B), cols], xl[pl.ds(s * B, B), cols] = split(w[b_index(q, s)])
        update(q, 0)

    def second_half(q):
        cols = columns(q)
        for s in range(2, 4):
            wait_other(1, b_index(q, s) - BASE[1])
        top = pl.ds(0, 2 * B)
        last = finish(w[b_index(q, 2)], w[b_index(q, 3)], xh[top, cols], xl[top, cols])
        for s in range(2, 4):
            xh[pl.ds(s * B, B), cols], xl[pl.ds(s * B, B), cols] = split(last[s - 2])
        update(q, 1)
        for s in range(4):

            @pl.when(row == s)
            def _(s=s):
                cv[pl.ds(0, B), cols] = w[b_index(q, s)] if s < 2 else last[s - 2]

    def step(u, carry):
        def blocks_at(rho, v):
            inside = jnp.logical_and(v >= 0, v < STEPS[rho])
            if rho == 0:
                return [(inside, v)]
            early = jnp.logical_and(v >= 0, v < 2)
            return [(inside, jnp.where(early, 2 * v, v + 2)), (early, 2 * v + 1)]

        for rho in range(2):
            for inside, n in blocks_at(rho, u):

                @pl.when(jnp.logical_and(is_root[rho], jnp.logical_and(inside, (n & 1) == core)))
                def _(rho=rho, n=n):
                    own(rho, n)

            for inside, n in blocks_at(rho, u - 2):
                odd = jnp.logical_and(core == 0, (n & 1) == 1)

                @pl.when(jnp.logical_and(is_root[rho], jnp.logical_and(inside, odd)))
                def _(rho=rho, n=n):
                    own_other(rho, n)

        for act in (forward, share):
            for rho in range(2):
                for il in range(2):
                    for inside, n in blocks_at(rho, u - LAG * depth[rho][il]):

                        @pl.when(jnp.logical_and(inside, jnp.logical_not(is_root[rho])))
                        def _(act=act, rho=rho, il=il, n=n):
                            act(rho, il, n)

        for rho in range(2):
            for il in range(2):
                inside, n = blocks_at(rho, u - LAG * depth[rho][il] - x_lag)[0]

                @pl.when(inside)
                def _(rho=rho, il=il, n=n):
                    x_arrive(rho, il, n)

        @pl.when(u == 0)
        def _():
            load_f.wait()

        @pl.when(u < 16)
        def _():
            rows = pl.ds(pl.multiple_of(u * 64, 64), 64)
            hi, lo = split(fv[rows, :])
            fh[rows, :] = hi
            fl[rows, :] = lo

        for n in range(NL[1]):

            @pl.when(u == WAIT + n // 2)
            def _(n=n):
                take_g(n)

        @pl.when(u == WAIT)
        def _():
            load_c.wait()

        g = u - WAIT

        @pl.when(jnp.logical_and((g & 1) == 1, jnp.logical_and(g >= 1, g < 8)))
        def _():
            first_half(g >> 1)

        second = jnp.logical_and((g & 1) == 0, jnp.logical_and(g >= 4, g < 9))

        @pl.when(jnp.logical_or(second, g == 9))
        def _():
            second_half((g - 3) >> 1)

        return carry

    lax.fori_loop(0, UNITS, step, 0)

    @pl.when(p == 0)
    def _():
        for s in range(4):
            xb[s] = w[b_index(qz, s), :, lanes]

    @pl.when(p != 0)
    def _():
        for s in range(4):
            for il in range(2):
                ref = x_piece(s, 2 * (1 - core) + il)
                remote(ref, ref, xss.at[s, il], xsb.at[s, il], sibling).wait_recv()

    parts = [split(xb[s]) for s in range(2)]
    hi, lo = (jnp.concatenate([parts[0][i], parts[1][i]], axis=0) for i in range(2))
    for s, v in enumerate([xb[0], xb[1], *finish(xb[2], xb[3], hi, lo)]):
        sbt[:, pl.ds(s * B, B)] = v.T
    load_p.wait()
    sh, sl = split(sbt[pl.ds(pl.multiple_of(core * 64, 64), 64), :])

    for q in range(4):
        cols = pl.ds(q * B, B)
        tv[:, cols] = pv[:, cols] - dot3(sh, sl, xh[:, cols], xl[:, cols])

    for rho in range(2):
        whole = w.at[pl.ds(0, NB[rho]), pl.ds(0, PIECE)]

        @pl.when(is_root[rho])
        def _(rho=rho):
            own_wait(0)
            own_wait(1)
            for j in range(NB[rho] // 2):
                whole_copy(0, 2 * j).wait_send()

        @pl.when(jnp.logical_not(is_root[rho]))
        def _(rho=rho, whole=whole):
            for il in range(2):
                for d in range(4):

                    @pl.when(((child[rho][il] >> d) & 1) == 1)
                    def _(il=il, d=d):
                        remote(whole, whole, child_sem.at[rho, il, d], rs.at[0, il], near_same[d]).wait_send()

                remote(whole, whole, sib_sem.at[rho, il], rs.at[0, il], sibling).wait_send()

    def x_sent(i, s, il):
        ref = x_piece(s, 2 * core + il)
        remote(ref, ref, xs.at[i, s, il], xr.at[s, il], sibling).wait_send()

    for s in range(4):
        for il in range(2):

            @pl.when(p == 0)
            def _(s=s, il=il):
                x_sent(0, s, il)
                x_sent(1, s, il)

            @pl.when(relays)
            def _(s=s, il=il):
                x_sent(0, s, il)

            @pl.when(p != 0)
            def _(s=s, il=il):
                ref = x_piece(s, 2 * core + il)
                remote(ref, ref, xss.at[s, il], xsb.at[s, il], sibling).wait_send()


def local(cross_cov, factor_cols, prior_cov):
    n = 1024
    dma = pltpu.SemaphoreType.DMA
    in_hbm = pl.BlockSpec(memory_space=pltpu.HBM)
    current, posterior = pl.pallas_call(
        kernel,
        out_shape=(pltpu.VMEM((n, n), F32), pltpu.VMEM((64, n), F32)),
        in_specs=[in_hbm] * 3,
        out_specs=(pl.BlockSpec(memory_space=pltpu.VMEM),) * 2,
        scratch_shapes=[
            pltpu.VMEM((BLOCKS, B, B), F32),
            pltpu.VMEM((n, n), F32),
            pltpu.VMEM((n, n), BF16),
            pltpu.VMEM((n, n), BF16),
            pltpu.VMEM((64, n), F32),
            pltpu.VMEM((n, n), BF16),
            pltpu.VMEM((n, n), BF16),
            pltpu.VMEM((2 * B, 2 * B), BF16),
            pltpu.VMEM((2 * B, 2 * B), BF16),
            pltpu.VMEM((4, B, B), BF16),
            pltpu.VMEM((B, B), F32),
            pltpu.VMEM((B, B), F32),
            pltpu.VMEM((4, B, 128), F32),
            pltpu.VMEM((128, n), F32),
            dma((BLOCKS, 2)),
            dma((BLOCKS, 2)),
            dma((2, 2, 4)),
            dma((2, 2)),
            dma((2, 4)),
            dma((6,)),
            dma((6,)),
            dma((3,)),
            dma((8,)),
            dma((4, 2)),
            dma((2, 4, 2)),
            dma((4, 2)),
            dma((4, 2)),
        ],
        compiler_params=pltpu.CompilerParams(
            collective_id=0, has_side_effects=True, vmem_limit_bytes=int(59.5 * 1024 * 1024)
        ),
        name="solve_update",
    )(cross_cov, factor_cols, prior_cov)
    return hand_on(current, posterior)


def hand_on_kernel(a_in, b_in, a_out, b_out, sem):
    rows = 256
    copies = [
        pltpu.make_async_copy(a_in.at[pl.ds(i * rows, rows)], a_out.at[pl.ds(i * rows, rows)], sem.at[i])
        for i in range(4)
    ]
    copies.append(pltpu.make_async_copy(b_in, b_out, sem.at[4]))
    for c in copies:
        c.start()
    for c in copies:
        c.wait()


def hand_on(current, posterior):
    return pl.pallas_call(
        hand_on_kernel,
        out_shape=(jax.ShapeDtypeStruct(current.shape, F32), jax.ShapeDtypeStruct(posterior.shape, F32)),
        in_specs=[pl.BlockSpec(memory_space=pltpu.VMEM)] * 2,
        out_specs=(pl.BlockSpec(memory_space=pltpu.HBM),) * 2,
        scratch_shapes=[pltpu.SemaphoreType.DMA((5,))],
        compiler_params=pltpu.CompilerParams(vmem_limit_bytes=8 * 1024 * 1024),
        name="hand_on",
    )(current, posterior)


def solution(mesh):
    placed = (P("row", "cand"), P("row", None), P("row", "cand"))
    return jax.shard_map(
        local,
        mesh=mesh,
        in_specs=placed,
        out_specs=(P("row", "cand"), P("row", "cand")),
        check_vma=False,
    )
```

```python
import functools

import jax
import jax.numpy as jnp
from jax import lax
from jax.experimental import pallas as pl
from jax.experimental.pallas import tpu as pltpu
from jax.sharding import PartitionSpec as P

MESH = pl.DeviceIdType.MESH
F32, BF16 = jnp.float32, jnp.bfloat16
HIGHEST = lax.Precision.HIGHEST
B = 256
PIECE = 64
LAG = 2

TREES = (
    (2, 112, 98, 82, 74, 62, 46, 22, 48, 96, 112, 98, 86, 66, 48, 37, 65, 93, 96, 112, 98, 81, 96, 49, 80, 96, 112, 98, 82, 72, 49, 65),
    (1, 21, 45, 61, 69, 81, 97, 112, 48, 38, 48, 64, 81, 97, 112, 96, 66, 50, 96, 82, 97, 112, 96, 94, 80, 66, 50, 73, 89, 97, 112, 96),
    (8, 48, 64, 80, 96, 80, 64, 48, 48, 96, 82, 96, 112, 96, 81, 96, 40, 48, 73, 88, 104, 90, 74, 48, 27, 45, 61, 68, 84, 70, 62, 46),
    (4, 56, 64, 80, 96, 80, 64, 56, 23, 41, 61, 77, 88, 76, 62, 42, 36, 80, 70, 85, 100, 84, 69, 80, 48, 64, 80, 96, 112, 96, 80, 64),
)
STEP = ((0, 1), (0, 7), (1, 0), (3, 0))
FIRST = (1, 0, 3, 2)
NL = (0, 4)
NB = (8, 12)
BASE = (0, 8)
BLOCKS = 20
WAIT = LAG * 7
STEPS = (8, 10)
UNITS = STEPS[1] + WAIT + 4


def b_index(q, s):
    return BASE[s // 2] + NL[s // 2] + 2 * q + s % 2


def split(x):
    hi = x.astype(BF16)
    return hi, (x - hi.astype(F32)).astype(BF16)


def dot(a, b):
    return jnp.dot(a, b, preferred_element_type=F32)


def dot3(ah, al, bh, bl):
    return dot(ah, bh) + (dot(ah, bl) + dot(al, bh))


def dotf(a, b):
    return jnp.dot(a, b, precision=HIGHEST, preferred_element_type=F32)


def invert_block(d):
    n = d.shape[0]
    ri = lax.broadcasted_iota(jnp.int32, (n, n), 0)
    ci = lax.broadcasted_iota(jnp.int32, (n, n), 1)
    same = ri == ci
    on_diag = jnp.where(same, d, 0.0)
    by_row = 1.0 / jnp.sum(on_diag, axis=1, keepdims=True)
    by_col = 1.0 / jnp.sum(on_diag, axis=0, keepdims=True)
    low = jnp.where(ri > ci, d, 0.0) * by_row
    inv = jnp.where(same, 1.0, 0.0) - jnp.where((ri >> 1) == (ci >> 1), low, 0.0)
    k = 1
    while 2 << k <= n:
        off = jnp.where(((ri >> (k + 1)) == (ci >> (k + 1))) & ((ri >> k) != (ci >> k)), low, 0.0)
        parts = split(inv)
        inv = inv - dot3(*split(dot3(*parts, *split(off))), *parts)
        k += 1
    return inv * by_col


def invert_lower(d):
    h = B // 2
    first, last = invert_block(d[:h, :h]), invert_block(d[h:, h:])
    corner = -dotf(dotf(last, d[h:, :h]), first)
    top = jnp.concatenate([first, jnp.zeros((h, h), F32)], axis=1)
    return jnp.concatenate([top, jnp.concatenate([corner, last], axis=1)], axis=0)


def kernel(
    c_hbm, f_hbm, p_hbm, cv, tv,
    w, fv, fh, fl, pv, xh, xl, gh, gl, dsp, dv, lv, xb, rb, sbt,
    rs, sb, child_sem, sib_sem, own_sem, pre_s, pre_r, load_sem, raw_sem, xr, xs, xsb, xss,
):
    row = lax.axis_index("row")
    x = lax.axis_index("cand")
    y = row >> 4
    z = (row >> 1) & 7
    core = row & 1

    def device(yy, zz, cc, xx=None):
        return ((yy & 3) * 16 + (zz & 7) * 2 + cc, x if xx is None else xx & 3)

    sibling = device(y, z, 1 - core)
    near = [[device(y + dy, z + dz, cc) for cc in range(2)] for dy, dz in STEP]
    near_same = [device(y + dy, z + dz, core) for dy, dz in STEP]
    beside = [device(y, z, core, x + dx) for dx in (1, 3)]

    def remote(src, dst, send_sem, recv_sem, to):
        return pltpu.make_async_remote_copy(
            src_ref=src, dst_ref=dst, send_sem=send_sem, recv_sem=recv_sem, device_id=to, device_id_type=MESH
        )

    load_f = pltpu.make_async_copy(f_hbm, fv, load_sem.at[0])
    load_c = pltpu.make_async_copy(c_hbm, cv, load_sem.at[1])
    load_p = pltpu.make_async_copy(p_hbm, pv, load_sem.at[2])

    def raw_copies(s):
        found = [(w.at[b_index(q, s)], c_hbm.at[pl.ds(0, B), pl.ds(q * B, B)]) for q in range(4)]
        for t in range(2 if s >= 2 else 0):
            found.append((w.at[BASE[1] + 2 * t + s % 2], f_hbm.at[pl.ds(0, B), pl.ds(t * B, B)]))
        if s % 2:
            found.append((lv, f_hbm.at[pl.ds(0, B), pl.ds((s - 1) * B, B)]))
        return [pltpu.make_async_copy(src, dst, raw_sem.at[i]) for i, (dst, src) in enumerate(found)]

    def load_d(s):
        return pltpu.make_async_copy(f_hbm.at[pl.ds(0, B), pl.ds(s * B, B)], dv, raw_sem.at[7])

    for s in range(4):

        @pl.when(row == s)
        def _(s=s):
            load_d(s).start()
            for c in raw_copies(s):
                c.start()

    barrier = pltpu.get_barrier_semaphore()
    for to in [t for pair in near for t in pair] + beside + [sibling]:
        pl.semaphore_signal(barrier, inc=1, device_id=to, device_id_type=MESH)
    load_f.start()
    load_c.start()
    load_p.start()

    for s in range(4):

        @pl.when(row == s)
        def _(s=s):
            load_d(s).wait()
            dsp[0], dsp[1] = split(invert_lower(dv[...]))
            for c in raw_copies(s):
                c.wait()
            if s % 2:
                dsp[2], dsp[3] = split(lv[...])

    def lookup(table, key):
        found = jnp.int32(0)
        for k, v in enumerate(table):
            found = jnp.where(key == k, v, found)
        return found

    is_root, depth, child = [], [], []
    for rho in range(2):
        idx = y * 8 + ((z - rho) & 7)
        merged = [TREES[2 * cc][k] + 128 * TREES[2 * cc + 1][k] for cc in range(2) for k in range(32)]
        v = lookup(merged, core * 32 + idx)
        is_root.append(idx == 0)
        depth.append(((v >> 4) & 7, v >> 11))
        child.append((v & 15, (v >> 7) & 15))

    p = (x - y) & 3
    qz = z >> 1
    lanes = pl.ds(pl.multiple_of((z & 1) * 128, 128), 128)
    relays = jnp.logical_or(jnp.logical_and(p == 1, core == 0), jnp.logical_and(p == 3, core == 1))
    onward = (beside[0][0], (x + jnp.where(core == 0, 1, 3)) & 3)
    x_lag = jnp.where(p == 2, 4, 2)

    pl.semaphore_wait(barrier, 11)

    def piece(b, tree):
        return w.at[b, pl.ds(pl.multiple_of(tree * 64, 64), PIECE)]

    def x_piece(s, tree):
        return xb.at[s, pl.ds(pl.multiple_of(tree * 64, 64), PIECE)]

    def needed(rho, n):
        m = n - NL[rho]
        return jnp.logical_and(m >= 0, (m >> 1) == qz), 2 * rho + (m & 1)

    def x_start(rho, il, n):
        hit, s = needed(rho, n)

        @pl.when(jnp.logical_and(p == 0, hit))
        def _():
            tree = 2 * core + il
            src = w.at[BASE[rho] + n, pl.ds(pl.multiple_of(tree * 64, 64), PIECE), lanes]
            for i in range(2):
                remote(src, x_piece(s, tree), xs.at[i, s, il], xr.at[s, il], beside[i]).start()

    def x_arrive(rho, il, n):
        hit, s = needed(rho, n)

        @pl.when(jnp.logical_and(p != 0, hit))
        def _():
            ref = x_piece(s, 2 * core + il)
            remote(ref, ref, xs.at[0, s, il], xr.at[s, il], sibling).wait_recv()

            @pl.when(relays)
            def _():
                remote(ref, ref, xs.at[0, s, il], xr.at[s, il], onward).start()

            remote(ref, ref, xss.at[s, il], xsb.at[s, il], sibling).start()

    def whole_copy(b, n):
        ref = w.at[b]
        return remote(ref, ref, pre_s.at[n >> 1], pre_r.at[n >> 1], sibling)

    def own_sends(b, slot):
        for tree in range(4):
            ref = w.at[b, pl.ds(64 * tree, PIECE)]
            yield remote(ref, ref, own_sem.at[slot, tree], rs.at[b, tree % 2], near[FIRST[tree]][tree // 2])

    def own_wait(slot):
        for copy in own_sends(0, slot):
            copy.wait_send()

    def own(rho, n):
        b = BASE[rho] + n
        j = n >> 1
        slot = j & 1

        @pl.when(core == 1)
        def _():
            whole_copy(b - 1, n).wait_recv()
            for il in range(2):
                x_start(rho, il, n - 1)
            w[b] = w[b] - dot3(dsp[2], dsp[3], *split(w[b - 1]))

        w[b] = dot3(dsp[0], dsp[1], *split(w[b]))
        whole_copy(b, n).start()

        @pl.when(j >= 2)
        def _():
            own_wait(slot)

        for copy in own_sends(b, slot):
            copy.start()
        for il in range(2):
            x_start(rho, il, n)

    def own_other(rho, n):
        whole_copy(BASE[rho] + n, n).wait_recv()
        for il in range(2):
            x_start(rho, il, n)

    def forward(rho, il, n):
        b = BASE[rho] + n
        ref = piece(b, 2 * core + il)
        remote(ref, ref, sib_sem.at[rho, il], rs.at[b, il], sibling).wait_recv()
        for d in range(4):

            @pl.when(((child[rho][il] >> d) & 1) == 1)
            def _(d=d):
                remote(ref, ref, child_sem.at[rho, il, d], rs.at[b, il], near_same[d]).start()

    def share(rho, il, n):
        b = BASE[rho] + n
        ref = piece(b, 2 * core + il)
        remote(ref, ref, sib_sem.at[rho, il], sb.at[b, il], sibling).start()
        x_start(rho, il, n)

    def wait_other(rho, n):
        b = BASE[rho] + n

        @pl.when(jnp.logical_not(is_root[rho]))
        def _():
            for il in range(2):
                ref = piece(b, 2 * (1 - core) + il)
                remote(ref, ref, sib_sem.at[rho, il], sb.at[b, il], sibling).wait_recv()

    def take_g(n):
        wait_other(1, n)
        half, t = n % 2, n // 2
        rows, cols = pl.ds(half * B, B), pl.ds(t * B, B)
        gh[rows, cols], gl[rows, cols] = split(w[BASE[1] + n])

    def finish(y2, y3, hi, lo):
        r = dot3(gh[...], gl[...], hi, lo)
        return y2 - r[:B], y3 - r[B:]

    def columns(q):
        return pl.ds(pl.multiple_of(q * B, B), B)

    def update(q, half):
        cols = columns(q)
        depth_part = pl.ds(half * 2 * B, 2 * B)
        for m in range(4):
            rows = pl.ds(m * B, B)
            cv[rows, cols] = cv[rows, cols] - dot3(
                fh[rows, depth_part], fl[rows, depth_part], xh[depth_part, cols], xl[depth_part, cols]
            )

    def first_half(q):
        cols = columns(q)
        for s in range(2):
            wait_other(0, 2 * q + s)
            xh[pl.ds(s * B, B), cols], xl[pl.ds(s * B, B), cols] = split(w[b_index(q, s)])
        update(q, 0)

    def second_half(q):
        cols = columns(q)
        for s in range(2, 4):
            wait_other(1, b_index(q, s) - BASE[1])
        top = pl.ds(0, 2 * B)
        last = finish(w[b_index(q, 2)], w[b_index(q, 3)], xh[top, cols], xl[top, cols])
        for s in range(2, 4):
            xh[pl.ds(s * B, B), cols], xl[pl.ds(s * B, B), cols] = split(last[s - 2])
        update(q, 1)
        for s in range(4):

            @pl.when(row == s)
            def _(s=s):
                cv[pl.ds(0, B), cols] = w[b_index(q, s)] if s < 2 else last[s - 2]

    def x_take(s):
        @pl.when(p == 0)
        def _():
            xb[s] = w[b_index(qz, s), :, lanes]

        @pl.when(p != 0)
        def _():
            for il in range(2):
                ref = x_piece(s, 2 * (1 - core) + il)
                remote(ref, ref, xss.at[s, il], xsb.at[s, il], sibling).wait_recv()

    mine = pl.ds(pl.multiple_of(core * 64, 64), 64)

    def downdate(before, half):
        part = pl.ds(half * 2 * B, 2 * B)
        sh, sl = split(sbt[mine, part])
        for q in range(4):
            cols = pl.ds(q * B, B)
            tv[:, cols] = before[:, cols] - dot3(sh, sl, xh[part, cols], xl[part, cols])

    def posterior_first():
        parts = []
        for s in range(2):
            x_take(s)
            parts.append(split(xb[s]))
            sbt[:, pl.ds(s * B, B)] = xb[s].T
        hi, lo = (jnp.concatenate([parts[0][i], parts[1][i]], axis=0) for i in range(2))
        rb[...] = dot3(gh[...], gl[...], hi, lo)
        load_p.wait()
        downdate(pv, 0)

    def posterior_second():
        for s in range(2, 4):
            x_take(s)
            sbt[:, pl.ds(s * B, B)] = (xb[s] - rb[pl.ds((s - 2) * B, B), :]).T
        downdate(tv, 1)

    def step(u, carry):
        def blocks_at(rho, v):
            inside = jnp.logical_and(v >= 0, v < STEPS[rho])
            if rho == 0:
                return [(inside, v)]
            early = jnp.logical_and(v >= 0, v < 2)
            return [(inside, jnp.where(early, 2 * v, v + 2)), (early, 2 * v + 1)]

        for rho in range(2):
            for inside, n in blocks_at(rho, u):

                @pl.when(jnp.logical_and(is_root[rho], jnp.logical_and(inside, (n & 1) == core)))
                def _(rho=rho, n=n):
                    own(rho, n)

            for inside, n in blocks_at(rho, u - 2):
                odd = jnp.logical_and(core == 0, (n & 1) == 1)

                @pl.when(jnp.logical_and(is_root[rho], jnp.logical_and(inside, odd)))
                def _(rho=rho, n=n):
                    own_other(rho, n)

        for act in (forward, share):
            for rho in range(2):
                for il in range(2):
                    for inside, n in blocks_at(rho, u - LAG * depth[rho][il]):

                        @pl.when(jnp.logical_and(inside, jnp.logical_not(is_root[rho])))
                        def _(act=act, rho=rho, il=il, n=n):
                            act(rho, il, n)

        for rho in range(2):
            for il in range(2):
                inside, n = blocks_at(rho, u - LAG * depth[rho][il] - x_lag)[0]

                @pl.when(inside)
                def _(rho=rho, il=il, n=n):
                    x_arrive(rho, il, n)

        @pl.when(u == 0)
        def _():
            load_f.wait()

        @pl.when(u < 16)
        def _():
            rows = pl.ds(pl.multiple_of(u * 64, 64), 64)
            hi, lo = split(fv[rows, :])
            fh[rows, :] = hi
            fl[rows, :] = lo

        for n in range(NL[1]):

            @pl.when(u == WAIT + n // 2)
            def _(n=n):
                take_g(n)

        @pl.when(u == WAIT)
        def _():
            load_c.wait()

        g = u - WAIT

        @pl.when(jnp.logical_and((g & 1) == 1, jnp.logical_and(g >= 1, g < 8)))
        def _():
            first_half(g >> 1)

        second = jnp.logical_and((g & 1) == 0, jnp.logical_and(g >= 4, g < 9))

        @pl.when(jnp.logical_or(second, g == 9))
        def _():
            second_half((g - 3) >> 1)

        @pl.when(g == 12)
        def _():
            posterior_first()

        return carry

    lax.fori_loop(0, UNITS, step, 0)

    posterior_second()

    for rho in range(2):
        whole = w.at[pl.ds(0, NB[rho]), pl.ds(0, PIECE)]

        @pl.when(is_root[rho])
        def _(rho=rho):
            own_wait(0)
            own_wait(1)
            for j in range(NB[rho] // 2):
                whole_copy(0, 2 * j).wait_send()

        @pl.when(jnp.logical_not(is_root[rho]))
        def _(rho=rho, whole=whole):
            for il in range(2):
                for d in range(4):

                    @pl.when(((child[rho][il] >> d) & 1) == 1)
                    def _(il=il, d=d):
                        remote(whole, whole, child_sem.at[rho, il, d], rs.at[0, il], near_same[d]).wait_send()

                remote(whole, whole, sib_sem.at[rho, il], rs.at[0, il], sibling).wait_send()

    def x_sent(i, s, il):
        ref = x_piece(s, 2 * core + il)
        remote(ref, ref, xs.at[i, s, il], xr.at[s, il], sibling).wait_send()

    for s in range(4):
        for il in range(2):

            @pl.when(p == 0)
            def _(s=s, il=il):
                x_sent(0, s, il)
                x_sent(1, s, il)

            @pl.when(relays)
            def _(s=s, il=il):
                x_sent(0, s, il)

            @pl.when(p != 0)
            def _(s=s, il=il):
                ref = x_piece(s, 2 * core + il)
                remote(ref, ref, xss.at[s, il], xsb.at[s, il], sibling).wait_send()


def local(cross_cov, factor_cols, prior_cov):
    n = 1024
    dma = pltpu.SemaphoreType.DMA
    in_hbm = pl.BlockSpec(memory_space=pltpu.HBM)
    current, posterior = pl.pallas_call(
        kernel,
        out_shape=(pltpu.VMEM((n, n), F32), pltpu.VMEM((64, n), F32)),
        in_specs=[in_hbm] * 3,
        out_specs=(pl.BlockSpec(memory_space=pltpu.VMEM),) * 2,
        scratch_shapes=[
            pltpu.VMEM((BLOCKS, B, B), F32),
            pltpu.VMEM((n, n), F32),
            pltpu.VMEM((n, n), BF16),
            pltpu.VMEM((n, n), BF16),
            pltpu.VMEM((64, n), F32),
            pltpu.VMEM((n, n), BF16),
            pltpu.VMEM((n, n), BF16),
            pltpu.VMEM((2 * B, 2 * B), BF16),
            pltpu.VMEM((2 * B, 2 * B), BF16),
            pltpu.VMEM((4, B, B), BF16),
            pltpu.VMEM((B, B), F32),
            pltpu.VMEM((B, B), F32),
            pltpu.VMEM((4, B, 128), F32),
            pltpu.VMEM((2 * B, 128), F32),
            pltpu.VMEM((128, n), F32),
            dma((BLOCKS, 2)),
            dma((BLOCKS, 2)),
            dma((2, 2, 4)),
            dma((2, 2)),
            dma((2, 4)),
            dma((6,)),
            dma((6,)),
            dma((3,)),
            dma((8,)),
            dma((4, 2)),
            dma((2, 4, 2)),
            dma((4, 2)),
            dma((4, 2)),
        ],
        compiler_params=pltpu.CompilerParams(
            collective_id=0, has_side_effects=True, vmem_limit_bytes=int(59.5 * 1024 * 1024)
        ),
        name="solve_update",
    )(cross_cov, factor_cols, prior_cov)
    return hand_on(current, posterior)


def hand_on_kernel(a_in, b_in, a_out, b_out, sem):
    rows = 256
    copies = [
        pltpu.make_async_copy(a_in.at[pl.ds(i * rows, rows)], a_out.at[pl.ds(i * rows, rows)], sem.at[i])
        for i in range(4)
    ]
    copies.append(pltpu.make_async_copy(b_in, b_out, sem.at[4]))
    for c in copies:
        c.start()
    for c in copies:
        c.wait()


def hand_on(current, posterior):
    return pl.pallas_call(
        hand_on_kernel,
        out_shape=(jax.ShapeDtypeStruct(current.shape, F32), jax.ShapeDtypeStruct(posterior.shape, F32)),
        in_specs=[pl.BlockSpec(memory_space=pltpu.VMEM)] * 2,
        out_specs=(pl.BlockSpec(memory_space=pltpu.HBM),) * 2,
        scratch_shapes=[pltpu.SemaphoreType.DMA((5,))],
        compiler_params=pltpu.CompilerParams(vmem_limit_bytes=8 * 1024 * 1024),
        name="hand_on",
    )(current, posterior)


def solution(mesh):
    placed = (P("row", "cand"), P("row", None), P("row", "cand"))
    return jax.shard_map(
        local,
        mesh=mesh,
        in_specs=placed,
        out_specs=(P("row", "cand"), P("row", "cand")),
        check_vma=False,
    )
```

```python
import functools

import jax
import jax.numpy as jnp
from jax import lax
from jax.experimental import pallas as pl
from jax.experimental.pallas import tpu as pltpu
from jax.sharding import PartitionSpec as P

MESH = pl.DeviceIdType.MESH
F32, BF16 = jnp.float32, jnp.bfloat16
HIGHEST = lax.Precision.HIGHEST
B = 256
PIECE = 64
LAG = 2

TREES = (
    (2, 112, 98, 82, 74, 62, 46, 22, 48, 96, 112, 98, 86, 66, 48, 37, 65, 93, 96, 112, 98, 81, 96, 49, 80, 96, 112, 98, 82, 72, 49, 65),
    (1, 21, 45, 61, 69, 81, 97, 112, 48, 38, 48, 64, 81, 97, 112, 96, 66, 50, 96, 82, 97, 112, 96, 94, 80, 66, 50, 73, 89, 97, 112, 96),
    (8, 48, 64, 80, 96, 80, 64, 48, 48, 96, 82, 96, 112, 96, 81, 96, 40, 48, 73, 88, 104, 90, 74, 48, 27, 45, 61, 68, 84, 70, 62, 46),
    (4, 56, 64, 80, 96, 80, 64, 56, 23, 41, 61, 77, 88, 76, 62, 42, 36, 80, 70, 85, 100, 84, 69, 80, 48, 64, 80, 96, 112, 96, 80, 64),
)
STEP = ((0, 1), (0, 7), (1, 0), (3, 0))
FIRST = (1, 0, 3, 2)
NL = (0, 4)
NB = (8, 12)
BASE = (0, 8)
BLOCKS = 20
WAIT = LAG * 7
STEPS = (8, 10)
UNITS = STEPS[1] + WAIT + 4


def b_index(q, s):
    return BASE[s // 2] + NL[s // 2] + 2 * q + s % 2


def split(x):
    hi = x.astype(BF16)
    return hi, (x - hi.astype(F32)).astype(BF16)


def dot(a, b):
    return jnp.dot(a, b, preferred_element_type=F32)


def dot3(ah, al, bh, bl):
    return dot(ah, bh) + (dot(ah, bl) + dot(al, bh))


def dotf(a, b):
    return jnp.dot(a, b, precision=HIGHEST, preferred_element_type=F32)


def invert_block(d):
    n = d.shape[0]
    ri = lax.broadcasted_iota(jnp.int32, (n, n), 0)
    ci = lax.broadcasted_iota(jnp.int32, (n, n), 1)
    same = ri == ci
    on_diag = jnp.where(same, d, 0.0)
    by_row = 1.0 / jnp.sum(on_diag, axis=1, keepdims=True)
    by_col = 1.0 / jnp.sum(on_diag, axis=0, keepdims=True)
    low = jnp.where(ri > ci, d, 0.0) * by_row
    inv = jnp.where(same, 1.0, 0.0) - jnp.where((ri >> 1) == (ci >> 1), low, 0.0)
    k = 1
    while 2 << k <= n:
        off = jnp.where(((ri >> (k + 1)) == (ci >> (k + 1))) & ((ri >> k) != (ci >> k)), low, 0.0)
        parts = split(inv)
        inv = inv - dot3(*split(dot3(*parts, *split(off))), *parts)
        k += 1
    return inv * by_col


def invert_lower(d):
    h = B // 2
    first, last = invert_block(d[:h, :h]), invert_block(d[h:, h:])
    corner = -dotf(dotf(last, d[h:, :h]), first)
    top = jnp.concatenate([first, jnp.zeros((h, h), F32)], axis=1)
    return jnp.concatenate([top, jnp.concatenate([corner, last], axis=1)], axis=0)


def kernel(
    c_hbm, f_hbm, p_hbm, cv, tv,
    w, fv, fh, fl, pv, xh, xl, gh, gl, dsp, dv, lv, xb, rb, sbt,
    rs, sb, child_sem, sib_sem, own_sem, pre_s, pre_r, load_sem, raw_sem, xr, xs, xsb, xss,
):
    row = lax.axis_index("row")
    x = lax.axis_index("cand")
    y = row >> 4
    z = (row >> 1) & 7
    core = row & 1

    def device(yy, zz, cc, xx=None):
        return ((yy & 3) * 16 + (zz & 7) * 2 + cc, x if xx is None else xx & 3)

    sibling = device(y, z, 1 - core)
    near = [[device(y + dy, z + dz, cc) for cc in range(2)] for dy, dz in STEP]
    near_same = [device(y + dy, z + dz, core) for dy, dz in STEP]
    beside = [device(y, z, core, x + dx) for dx in (1, 3)]

    def remote(src, dst, send_sem, recv_sem, to):
        return pltpu.make_async_remote_copy(
            src_ref=src, dst_ref=dst, send_sem=send_sem, recv_sem=recv_sem, device_id=to, device_id_type=MESH
        )

    load_f = pltpu.make_async_copy(f_hbm, fv, load_sem.at[0])
    load_c = pltpu.make_async_copy(c_hbm, cv, load_sem.at[1])
    load_p = pltpu.make_async_copy(p_hbm, pv, load_sem.at[2])

    def raw_copies(s):
        found = [(w.at[b_index(q, s)], c_hbm.at[pl.ds(0, B), pl.ds(q * B, B)]) for q in range(4)]
        for t in range(2 if s >= 2 else 0):
            found.append((w.at[BASE[1] + 2 * t + s % 2], f_hbm.at[pl.ds(0, B), pl.ds(t * B, B)]))
        if s % 2:
            found.append((lv, f_hbm.at[pl.ds(0, B), pl.ds((s - 1) * B, B)]))
        return [pltpu.make_async_copy(src, dst, raw_sem.at[i]) for i, (dst, src) in enumerate(found)]

    def load_d(s):
        return pltpu.make_async_copy(f_hbm.at[pl.ds(0, B), pl.ds(s * B, B)], dv, raw_sem.at[7])

    for s in range(4):

        @pl.when(row == s)
        def _(s=s):
            load_d(s).start()
            for c in raw_copies(s):
                c.start()

    barrier = pltpu.get_barrier_semaphore()
    for to in [t for pair in near for t in pair] + beside + [sibling]:
        pl.semaphore_signal(barrier, inc=1, device_id=to, device_id_type=MESH)
    load_f.start()
    load_c.start()
    load_p.start()

    for s in range(4):

        @pl.when(row == s)
        def _(s=s):
            load_d(s).wait()
            dsp[0], dsp[1] = split(invert_lower(dv[...]))
            for c in raw_copies(s):
                c.wait()
            if s % 2:
                dsp[2], dsp[3] = split(lv[...])

    def lookup(table, key):
        found = jnp.int32(0)
        for k, v in enumerate(table):
            found = jnp.where(key == k, v, found)
        return found

    is_root, depth, child = [], [], []
    for rho in range(2):
        idx = y * 8 + ((z - rho) & 7)
        merged = [TREES[2 * cc][k] + 128 * TREES[2 * cc + 1][k] for cc in range(2) for k in range(32)]
        v = lookup(merged, core * 32 + idx)
        is_root.append(idx == 0)
        depth.append(((v >> 4) & 7, v >> 11))
        child.append((v & 15, (v >> 7) & 15))

    p = (x - y) & 3
    qz = z >> 1
    lanes = pl.ds(pl.multiple_of((z & 1) * 128, 128), 128)
    relays = jnp.logical_or(jnp.logical_and(p == 1, core == 0), jnp.logical_and(p == 3, core == 1))
    onward = (beside[0][0], (x + jnp.where(core == 0, 1, 3)) & 3)
    x_lag = jnp.where(p == 2, 4, 2)

    pl.semaphore_wait(barrier, 11)

    def piece(b, tree):
        return w.at[b, pl.ds(pl.multiple_of(tree * 64, 64), PIECE)]

    def x_piece(s, tree):
        return xb.at[s, pl.ds(pl.multiple_of(tree * 64, 64), PIECE)]

    def needed(rho, n):
        m = n - NL[rho]
        return jnp.logical_and(m >= 0, (m >> 1) == qz), 2 * rho + (m & 1)

    def x_start(rho, il, n):
        hit, s = needed(rho, n)

        @pl.when(jnp.logical_and(p == 0, hit))
        def _():
            tree = 2 * core + il
            src = w.at[BASE[rho] + n, pl.ds(pl.multiple_of(tree * 64, 64), PIECE), lanes]
            for i in range(2):
                remote(src, x_piece(s, tree), xs.at[i, s, il], xr.at[s, il], beside[i]).start()

    def x_arrive(rho, il, n):
        hit, s = needed(rho, n)

        @pl.when(jnp.logical_and(p != 0, hit))
        def _():
            ref = x_piece(s, 2 * core + il)
            remote(ref, ref, xs.at[0, s, il], xr.at[s, il], sibling).wait_recv()

            @pl.when(relays)
            def _():
                remote(ref, ref, xs.at[0, s, il], xr.at[s, il], onward).start()

            remote(ref, ref, xss.at[s, il], xsb.at[s, il], sibling).start()

    def whole_copy(b, n):
        ref = w.at[b]
        return remote(ref, ref, pre_s.at[n >> 1], pre_r.at[n >> 1], sibling)

    def own_sends(b, slot):
        for tree in range(4):
            ref = w.at[b, pl.ds(64 * tree, PIECE)]
            yield remote(ref, ref, own_sem.at[slot, tree], rs.at[b, tree % 2], near[FIRST[tree]][tree // 2])

    def own_wait(slot):
        for copy in own_sends(0, slot):
            copy.wait_send()

    def own(rho, n):
        b = BASE[rho] + n
        j = n >> 1
        slot = j & 1

        @pl.when(core == 1)
        def _():
            whole_copy(b - 1, n).wait_recv()
            for il in range(2):
                x_start(rho, il, n - 1)
            w[b] = w[b] - dot3(dsp[2], dsp[3], *split(w[b - 1]))

        w[b] = dot3(dsp[0], dsp[1], *split(w[b]))
        whole_copy(b, n).start()

        @pl.when(j >= 2)
        def _():
            own_wait(slot)

        for copy in own_sends(b, slot):
            copy.start()
        for il in range(2):
            x_start(rho, il, n)

    def own_other(rho, n):
        whole_copy(BASE[rho] + n, n).wait_recv()
        for il in range(2):
            x_start(rho, il, n)

    def forward(rho, il, n):
        b = BASE[rho] + n
        ref = piece(b, 2 * core + il)
        remote(ref, ref, sib_sem.at[rho, il], rs.at[b, il], sibling).wait_recv()
        for d in range(4):

            @pl.when(((child[rho][il] >> d) & 1) == 1)
            def _(d=d):
                remote(ref, ref, child_sem.at[rho, il, d], rs.at[b, il], near_same[d]).start()

    def share(rho, il, n):
        b = BASE[rho] + n
        ref = piece(b, 2 * core + il)
        remote(ref, ref, sib_sem.at[rho, il], sb.at[b, il], sibling).start()
        x_start(rho, il, n)

    def wait_other(rho, n):
        b = BASE[rho] + n

        @pl.when(jnp.logical_not(is_root[rho]))
        def _():
            for il in range(2):
                ref = piece(b, 2 * (1 - core) + il)
                remote(ref, ref, sib_sem.at[rho, il], sb.at[b, il], sibling).wait_recv()

    def take_g(n):
        wait_other(1, n)
        half, t = n % 2, n // 2
        rows, cols = pl.ds(half * B, B), pl.ds(t * B, B)
        gh[rows, cols], gl[rows, cols] = split(w[BASE[1] + n])

    def finish(y2, y3, hi, lo):
        r = dot3(gh[...], gl[...], hi, lo)
        return y2 - r[:B], y3 - r[B:]

    def columns(q):
        return pl.ds(pl.multiple_of(q * B, B), B)

    def update(q, half):
        cols = columns(q)
        depth_part = pl.ds(half * 2 * B, 2 * B)
        for m in range(4):
            rows = pl.ds(m * B, B)
            cv[rows, cols] = cv[rows, cols] - dot3(
                fh[rows, depth_part], fl[rows, depth_part], xh[depth_part, cols], xl[depth_part, cols]
            )

    def first_half(q):
        cols = columns(q)
        for s in range(2):
            wait_other(0, 2 * q + s)
            xh[pl.ds(s * B, B), cols], xl[pl.ds(s * B, B), cols] = split(w[b_index(q, s)])
        update(q, 0)

    def second_half(q):
        cols = columns(q)
        for s in range(2, 4):
            wait_other(1, b_index(q, s) - BASE[1])
        top = pl.ds(0, 2 * B)
        last = finish(w[b_index(q, 2)], w[b_index(q, 3)], xh[top, cols], xl[top, cols])
        for s in range(2, 4):
            xh[pl.ds(s * B, B), cols], xl[pl.ds(s * B, B), cols] = split(last[s - 2])
        update(q, 1)
        for s in range(4):

            @pl.when(row == s)
            def _(s=s):
                cv[pl.ds(0, B), cols] = w[b_index(q, s)] if s < 2 else last[s - 2]

    def x_take(s):
        @pl.when(p == 0)
        def _():
            xb[s] = w[b_index(qz, s), :, lanes]

        @pl.when(p != 0)
        def _():
            for il in range(2):
                ref = x_piece(s, 2 * (1 - core) + il)
                remote(ref, ref, xss.at[s, il], xsb.at[s, il], sibling).wait_recv()

    mine = pl.ds(pl.multiple_of(core * 64, 64), 64)

    def downdate(before, half):
        part = pl.ds(half * 2 * B, 2 * B)
        sh, sl = split(sbt[mine, part])
        for q in range(4):
            cols = pl.ds(q * B, B)
            tv[:, cols] = before[:, cols] - dot3(sh, sl, xh[part, cols], xl[part, cols])

    def posterior_first():
        parts = []
        for s in range(2):
            x_take(s)
            parts.append(split(xb[s]))
            sbt[:, pl.ds(s * B, B)] = xb[s].T
        hi, lo = (jnp.concatenate([parts[0][i], parts[1][i]], axis=0) for i in range(2))
        rb[...] = dot3(gh[...], gl[...], hi, lo)
        load_p.wait()
        downdate(pv, 0)

    def posterior_second():
        for s in range(2, 4):
            x_take(s)
            sbt[:, pl.ds(s * B, B)] = (xb[s] - rb[pl.ds((s - 2) * B, B), :]).T
        downdate(tv, 1)

    def step(u, carry):
        def blocks_at(rho, v):
            inside = jnp.logical_and(v >= 0, v < STEPS[rho])
            if rho == 0:
                return [(inside, v)]
            early = jnp.logical_and(v >= 0, v < 2)
            return [(inside, jnp.where(early, 2 * v, v + 2)), (early, 2 * v + 1)]

        for rho in range(2):
            for inside, n in blocks_at(rho, u):

                @pl.when(jnp.logical_and(is_root[rho], jnp.logical_and(inside, (n & 1) == core)))
                def _(rho=rho, n=n):
                    own(rho, n)

            for inside, n in blocks_at(rho, u - 2):
                odd = jnp.logical_and(core == 0, (n & 1) == 1)

                @pl.when(jnp.logical_and(is_root[rho], jnp.logical_and(inside, odd)))
                def _(rho=rho, n=n):
                    own_other(rho, n)

        for act in (forward, share):
            for rho in range(2):
                for il in range(2):
                    for inside, n in blocks_at(rho, u - LAG * depth[rho][il]):

                        @pl.when(jnp.logical_and(inside, jnp.logical_not(is_root[rho])))
                        def _(act=act, rho=rho, il=il, n=n):
                            act(rho, il, n)

        @pl.when(u == 0)
        def _():
            load_f.wait()

        @pl.when(u < 16)
        def _():
            rows = pl.ds(pl.multiple_of(u * 64, 64), 64)
            hi, lo = split(fv[rows, :])
            fh[rows, :] = hi
            fl[rows, :] = lo

        for n in range(NL[1]):

            @pl.when(u == WAIT + n // 2)
            def _(n=n):
                take_g(n)

        @pl.when(u == WAIT)
        def _():
            load_c.wait()

        g = u - WAIT

        @pl.when(jnp.logical_and((g & 1) == 1, jnp.logical_and(g >= 1, g < 8)))
        def _():
            first_half(g >> 1)

        second = jnp.logical_and((g & 1) == 0, jnp.logical_and(g >= 4, g < 9))

        @pl.when(jnp.logical_or(second, g == 9))
        def _():
            second_half((g - 3) >> 1)

        @pl.when(g == 12)
        def _():
            posterior_first()

        for rho in range(2):
            for il in range(2):
                inside, n = blocks_at(rho, u - LAG * depth[rho][il] - x_lag)[0]

                @pl.when(inside)
                def _(rho=rho, il=il, n=n):
                    x_arrive(rho, il, n)

        return carry

    lax.fori_loop(0, UNITS, step, 0)

    posterior_second()

    for rho in range(2):
        whole = w.at[pl.ds(0, NB[rho]), pl.ds(0, PIECE)]

        @pl.when(is_root[rho])
        def _(rho=rho):
            own_wait(0)
            own_wait(1)
            for j in range(NB[rho] // 2):
                whole_copy(0, 2 * j).wait_send()

        @pl.when(jnp.logical_not(is_root[rho]))
        def _(rho=rho, whole=whole):
            for il in range(2):
                for d in range(4):

                    @pl.when(((child[rho][il] >> d) & 1) == 1)
                    def _(il=il, d=d):
                        remote(whole, whole, child_sem.at[rho, il, d], rs.at[0, il], near_same[d]).wait_send()

                remote(whole, whole, sib_sem.at[rho, il], rs.at[0, il], sibling).wait_send()

    def x_sent(i, s, il):
        ref = x_piece(s, 2 * core + il)
        remote(ref, ref, xs.at[i, s, il], xr.at[s, il], sibling).wait_send()

    for s in range(4):
        for il in range(2):

            @pl.when(p == 0)
            def _(s=s, il=il):
                x_sent(0, s, il)
                x_sent(1, s, il)

            @pl.when(relays)
            def _(s=s, il=il):
                x_sent(0, s, il)

            @pl.when(p != 0)
            def _(s=s, il=il):
                ref = x_piece(s, 2 * core + il)
                remote(ref, ref, xss.at[s, il], xsb.at[s, il], sibling).wait_send()


def local(cross_cov, factor_cols, prior_cov):
    n = 1024
    dma = pltpu.SemaphoreType.DMA
    in_hbm = pl.BlockSpec(memory_space=pltpu.HBM)
    current, posterior = pl.pallas_call(
        kernel,
        out_shape=(pltpu.VMEM((n, n), F32), pltpu.VMEM((64, n), F32)),
        in_specs=[in_hbm] * 3,
        out_specs=(pl.BlockSpec(memory_space=pltpu.VMEM),) * 2,
        scratch_shapes=[
            pltpu.VMEM((BLOCKS, B, B), F32),
            pltpu.VMEM((n, n), F32),
            pltpu.VMEM((n, n), BF16),
            pltpu.VMEM((n, n), BF16),
            pltpu.VMEM((64, n), F32),
            pltpu.VMEM((n, n), BF16),
            pltpu.VMEM((n, n), BF16),
            pltpu.VMEM((2 * B, 2 * B), BF16),
            pltpu.VMEM((2 * B, 2 * B), BF16),
            pltpu.VMEM((4, B, B), BF16),
            pltpu.VMEM((B, B), F32),
            pltpu.VMEM((B, B), F32),
            pltpu.VMEM((4, B, 128), F32),
            pltpu.VMEM((2 * B, 128), F32),
            pltpu.VMEM((128, n), F32),
            dma((BLOCKS, 2)),
            dma((BLOCKS, 2)),
            dma((2, 2, 4)),
            dma((2, 2)),
            dma((2, 4)),
            dma((6,)),
            dma((6,)),
            dma((3,)),
            dma((8,)),
            dma((4, 2)),
            dma((2, 4, 2)),
            dma((4, 2)),
            dma((4, 2)),
        ],
        compiler_params=pltpu.CompilerParams(
            collective_id=0, has_side_effects=True, vmem_limit_bytes=int(59.5 * 1024 * 1024)
        ),
        name="solve_update",
    )(cross_cov, factor_cols, prior_cov)
    return hand_on(current, posterior)


def hand_on_kernel(a_in, b_in, a_out, b_out, sem):
    rows = 256
    copies = [
        pltpu.make_async_copy(a_in.at[pl.ds(i * rows, rows)], a_out.at[pl.ds(i * rows, rows)], sem.at[i])
        for i in range(4)
    ]
    copies.append(pltpu.make_async_copy(b_in, b_out, sem.at[4]))
    for c in copies:
        c.start()
    for c in copies:
        c.wait()


def hand_on(current, posterior):
    return pl.pallas_call(
        hand_on_kernel,
        out_shape=(jax.ShapeDtypeStruct(current.shape, F32), jax.ShapeDtypeStruct(posterior.shape, F32)),
        in_specs=[pl.BlockSpec(memory_space=pltpu.VMEM)] * 2,
        out_specs=(pl.BlockSpec(memory_space=pltpu.HBM),) * 2,
        scratch_shapes=[pltpu.SemaphoreType.DMA((5,))],
        compiler_params=pltpu.CompilerParams(vmem_limit_bytes=8 * 1024 * 1024),
        name="hand_on",
    )(current, posterior)


def solution(mesh):
    placed = (P("row", "cand"), P("row", None), P("row", "cand"))
    return jax.shard_map(
        local,
        mesh=mesh,
        in_specs=placed,
        out_specs=(P("row", "cand"), P("row", "cand")),
        check_vma=False,
    )
```
